512 devices in a mesh: grp: 16 (over y_lo, x, core), fsdp: 32 (over z, y_hi).
Axes of the slice: x: 4, y: 4 (y_hi: 2, y_lo: 2; y = y_hi * 2 + y_lo), z: 16, core: 2. Of those that a mesh axis runs over, the one named last changes fastest.
Arguments:
- raw_clips: bfloat16 [16, 1024, 8, 2048], P('grp', 'fsdp'), may hold values from -6 to 6
- clip_lengths: int32 [16, 32, 32], P('grp', 'fsdp'), may hold values from 1 to 8, 160 in all within a row
- clip_routes: int32 [16, 1024, 1], P('grp', 'fsdp'), may hold values from 0 to 31; in each aligned block of 32 rows (0 to 31, 32 to 63, ..., all dimensions but the last counted through in order) at most 2 rows name the same one
- w_spectral: bfloat16 [1024, 4096], P('fsdp', 'grp'), may hold values from -0.1875 to 0.1875
- norm_gain: float32 [4096], replicated, may hold values from 0.25 to 1.75
- room_heads: bfloat16 [32, 4096, 256], P('fsdp'), may hold values from -0.09375 to 0.09375
Outputs:
- decay_curves: bfloat16 [16, 1024, 8, 256], P('grp', 'fsdp')
The draws below stay inside these ranges and needn't reach their ends.
Inputs may be any that keep to these rules, and one draw needn't show every extreme that they name: `clip_routes`: among the 32 clips of one device, no room head is named more than 2 times, and in every draw some device names some room head exactly 2 times; every room head is named by some clip. `clip_lengths`: the 32 lengths of one device sum to 160, and the longest of them is exactly 8.
All inputs are finite; a program needn't handle non-finite values.
Results may differ from the reference program's by a relative error of at most 0.007.
Values may be sent and summed in bfloat16 or wider, within the bound.
A program may use at most 64 MiB of HBM per device.

```python
import math
import jax
import jax.numpy as jnp
import numpy as np
from jax import lax

D = 4096
BINS = 1024
CURVE = 256
CLIP_MAX = 8
SLOTS = 2
WIN = 2048
CLIPS_DEV = 32
CLIPS = 1024
EXPERTS = 32
N_GRP = 16
N_FSDP = 32


def steps_of(own_key, extent, shards, low, top_value):
    factor_of = 1.0
    for dim, blocks in shards:
        steps = jax.random.uniform(jax.random.fold_in(jax.random.fold_in(own_key, 6), dim), (blocks,), jnp.float32, low / len(shards), top_value / len(shards))
        factor_of = factor_of * jnp.repeat(jnp.exp(steps), extent[dim] // blocks).reshape((-1,) + (1,) * (len(extent) - 1 - dim))
    return factor_of


def length_profile(count, total, bound, lean):
    portions = [(1 << 20) // math.isqrt(grade ** lean) + 1 for grade in range(2, count + 1)]
    spare, holding = total - bound - (count - 1), [1] * (count - 1)
    while spare > 0:
        movable = [i for i in range(count - 1) if holding[i] < bound]
        mass, left = sum([portions[i] for i in movable]), spare
        for i in movable:
            addition = min(bound - holding[i], max(1, left * portions[i] // mass), spare)
            holding[i] = holding[i] + addition
            spare = spare - addition
    return np.array([bound] + holding)


def uneven_parts(stream_key, number_of, total, most, skew):
    if number_of == 2:
        one = jax.random.randint(stream_key, (), max(1, total - most), min(most, total - 1) + 1)
        return jnp.stack([one, total - one])
    lengths = jnp.asarray(length_profile(number_of, total, most, skew), jnp.int32)
    pairs = (number_of - 1) // 2
    donor, sink = lengths[1:1 + 2 * pairs:2], lengths[2:2 + 2 * pairs:2]
    room = jnp.minimum(donor - 1, most - sink)
    passed = jax.random.randint(jax.random.fold_in(stream_key, 1), (pairs,), 0, 1 << 20) % (room + 1)
    lengths = lengths.at[1:1 + 2 * pairs:2].set(donor - passed).at[2:2 + 2 * pairs:2].set(sink + passed)
    return lengths[jax.random.permutation(jax.random.fold_in(stream_key, 2), number_of)]


def shared_out(rng, own, number, rows, number_of, top, bound, lean):
    sequence = jax.random.permutation(rng, number_of)
    packed, usual = load_shares(number_of, rows * top, bound, lean, True), load_shares(number_of, rows * top, bound, lean, False)
    places = jnp.arange(number_of)

    def named(sizes, offset_by):
        used = int((sizes > 0).sum())
        fixed = max(1, used // 4)
        passed = fixed + (places - fixed + offset_by * (used - fixed)) % max(1, number_of - fixed)
        return jnp.zeros((number_of,), jnp.int32).at[sequence[jnp.where(places < fixed, places, passed)]].set(jnp.asarray(sizes, jnp.int32))

    sizes = jnp.where(number % 4 == 0, named(packed, number // 4), named(usual, number - number // 4 - 1))
    mixed = jax.random.permutation(jax.random.fold_in(own, 3), number_of)
    source_of, taker = mixed[0:number_of // 2 * 2:2], mixed[1:number_of // 2 * 2:2]
    margin = jnp.minimum(sizes[source_of] - 1, bound - sizes[taker]) // 2
    margin = jnp.where((source_of == sequence[0]) | (taker == sequence[0]) | (sizes[taker] == 0), 0, jnp.maximum(margin, 0))
    passed = jax.random.randint(jax.random.fold_in(own, 4), (number_of // 2,), 0, 1 << 20) % (margin + 1)
    sizes = sizes.at[source_of].add(-passed).at[taker].add(passed)
    members = jnp.searchsorted(jnp.cumsum(sizes), jnp.arange(rows * top), side="right").astype(jnp.int32)
    table = members.reshape(top, rows).T
    table = table[jax.random.permutation(jax.random.fold_in(own, 1), rows)]
    offset_by = jax.random.randint(jax.random.fold_in(own, 2), (rows, 1), 0, top)
    return jnp.take_along_axis(table, (jnp.arange(top)[None, :] + offset_by) % top, axis=1)


def load_shares(number_of, total, bound, slope, full):
    portions = [(1 << 20) // math.isqrt(grade ** slope) + 1 for grade in range(1, number_of + 1)]
    largest = bound if full else min(bound, max(-(-total // number_of), total * portions[0] // sum(portions)))
    least = 1 if total - largest >= number_of - 1 else 0
    counts, spare = [largest] + [least] * (number_of - 1), total - largest - least * (number_of - 1)
    while spare > 0:
        movable = [i for i in range(1, number_of) if counts[i] < largest] or [i for i in range(1, number_of) if counts[i] < bound]
        whole, budget = sum([portions[i] for i in movable]), spare
        for i in movable:
            more = min(bound - counts[i], max(1, budget * portions[i] // whole), spare)
            counts[i] = counts[i] + more
            spare = spare - more
    return np.array(counts)


def centred(key, shape, scale, limit, shards=(), held_as=jnp.bfloat16):
    result = scale * jax.random.normal(key, shape, jnp.float32)
    if shards:
        result = result * steps_of(key, shape, shards, -0.22, 0.18)
    return jnp.clip(result, -limit, limit).astype(held_as)


def setup_inputs(seed: int = 0) -> dict:
    key_of = jax.random.split(jax.random.key(seed), 7)
    raw_clips = centred(key_of[0], (N_GRP, CLIPS, CLIP_MAX, WIN), 1.0, 6.0, ((0, 16), (1, 32)))
    clip_lengths = jax.vmap(lambda own: uneven_parts(own, CLIPS_DEV, CLIPS_DEV * CLIP_MAX * 5 // 8, CLIP_MAX, 2))(jax.random.split(key_of[1], N_GRP * N_FSDP)).reshape((N_GRP, N_FSDP, CLIPS_DEV)).astype(jnp.int32)
    clip_routes_keys = jax.random.split(jax.random.fold_in(key_of[2], 1), N_GRP * CLIPS // CLIPS_DEV)
    clip_routes_turns = jax.random.permutation(jax.random.fold_in(key_of[2], 3), N_GRP * CLIPS // CLIPS_DEV)
    clip_routes = jax.vmap(lambda own, number: shared_out(jax.random.fold_in(key_of[2], 2), own, number, CLIPS_DEV, N_FSDP, 1, SLOTS, 2))(clip_routes_keys, clip_routes_turns).reshape((N_GRP, CLIPS, 1))
    w_spectral = centred(key_of[3], (BINS, D), BINS ** -0.5, 0.1875, ((0, 32), (1, 16)))
    norm_gain = jnp.clip(1.0 + 0.15 * jax.random.normal(key_of[4], (D,), jnp.float32), 0.25, 1.75)
    room_heads = centred(key_of[5], (EXPERTS, D, CURVE), D ** -0.5, 0.09375, ((0, 32),))
    return {"raw_clips": raw_clips, "clip_lengths": clip_lengths, "clip_routes": clip_routes, "w_spectral": w_spectral, "norm_gain": norm_gain, "room_heads": room_heads}


norm_epsilon = 1e-05

def spectral_table(window):
    sample_idx = jnp.arange(window, dtype=jnp.int32)
    bin_idx = jnp.arange(window // 2, dtype=jnp.int32)
    products = sample_idx[:, None] * bin_idx[None, :] % window
    angles = products.astype(jnp.float32) * (2.0 * math.pi / window)
    taper_window = 0.5 - 0.5 * jnp.cos(sample_idx.astype(jnp.float32) * (2.0 * math.pi / window))
    cosines = taper_window[:, None] * jnp.cos(angles)
    sines = -taper_window[:, None] * jnp.sin(angles)
    return jnp.concatenate([cosines, sines], axis=1).astype(jnp.bfloat16)

def log_energy(frames, dft_table):
    window = frames.shape[1]
    bin_count = window // 2
    spectra = jnp.dot(frames, dft_table, preferred_element_type=jnp.float32)
    real_part = spectra[:, :bin_count]
    imag_part = spectra[:, bin_count:]
    return jnp.log1p((real_part * real_part + imag_part * imag_part) / window)

def center_clips(features, lengths_now):
    frame_slots = features.shape[1]
    alive_mask = (jnp.arange(frame_slots, dtype=jnp.int32)[None, :] < lengths_now[:, None]).astype(jnp.float32)
    clip_mean = lax.optimization_barrier(jnp.sum(features * alive_mask[:, :, None], axis=1)) / lengths_now[:, None].astype(jnp.float32)
    return ((features - clip_mean[:, None, :]).astype(jnp.bfloat16), alive_mask)

def rms_normed(projected, norm_gain):
    mean_square = lax.optimization_barrier(jnp.mean(projected * projected, axis=-1, keepdims=True))
    return (projected * lax.rsqrt(mean_square + norm_epsilon) * norm_gain).astype(jnp.bfloat16)

def reference(raw_clips, clip_lengths, clip_routes, w_spectral, norm_gain, room_heads):
    window = raw_clips.shape[3]
    frame_slots = raw_clips.shape[2]
    dft_table = spectral_table(window)

    def one_group(operands):
        raw_group, length_group, route_group = operands
        clip_count = raw_group.shape[0]
        features = log_energy(raw_group.reshape(-1, window), dft_table).reshape(clip_count, frame_slots, -1)
        lengths_now = length_group.reshape(clip_count)
        centered, alive_mask = center_clips(features, lengths_now)
        projected = jnp.dot(centered.reshape(clip_count * frame_slots, -1), w_spectral, preferred_element_type=jnp.float32)
        normed = rms_normed(projected, norm_gain).reshape(clip_count, frame_slots, -1)

        def one_clip(clip_operands):
            clip_rows, route_now = clip_operands
            head = lax.dynamic_index_in_dim(room_heads, route_now, 0, keepdims=False)
            return jnp.dot(clip_rows, head, preferred_element_type=jnp.float32).astype(jnp.bfloat16)
        curves = lax.map(one_clip, (normed, route_group[:, 0].astype(jnp.int32)))
        return curves * alive_mask[:, :, None].astype(jnp.bfloat16)
    return lax.map(one_group, (raw_clips, clip_lengths, clip_routes))
```

```python
import functools
import math

import jax
import jax.numpy as jnp
from jax import lax
from jax.experimental import pallas as pl
from jax.experimental.pallas import tpu as pltpu
from jax.sharding import PartitionSpec as P

SLOTS = 2
MESH = pl.DeviceIdType.MESH
norm_epsilon = 1e-05


def remote(src, dst, send_sem, recv_sem, device):
    return pltpu.make_async_remote_copy(
        src_ref=src,
        dst_ref=dst,
        send_sem=send_sem,
        recv_sem=recv_sem,
        device_id=device,
        device_id_type=MESH,
    )


def loop(low, high, step):
    def body(i, carry):
        step(i)
        return carry

    lax.fori_loop(low, high, body, 0)


def kernel(
    n,
    raw_ref, w_ref, gain_ref, head_ref, srow_ref, scol_ref, live_ref,
    out_ref,
    tab, trc, trs, c_own, c_pair, cs, cr, wz, wr, ws, mc, mz, mr, gp, gz, gs, gf, y, yr, ms_send, ms_recv,
    w1s, w1r, wss, wsr, w2s, w2r, m1s, m1r, m2s, m2r, g1s, g1r, g2s, g2r, c1s, c1r, c3s, c3r, xs, xr,
):
    rooms = 2 * n
    rows, window = raw_ref.shape
    bins = c_own.shape[1]
    half = bins // 2
    rb = w_ref.shape[0]
    g, f = lax.axis_index("grp"), lax.axis_index("fsdp")
    z, h = f // 2, lax.rem(f, 2)
    core = lax.rem(g, 2)
    me = 2 * g + h
    pair = (g + 1 - 2 * core, f)

    def in_plane(q):
        return (q // 2, 2 * z + lax.rem(q, 2))

    def in_column(q):
        return (g, 2 * q + h)

    barrier = pltpu.get_barrier_semaphore()

    def greet_plane(d):
        pl.semaphore_signal(barrier, inc=1, device_id=in_plane(lax.rem(me + d, rooms)), device_id_type=MESH)

    def greet_column(d):
        pl.semaphore_signal(barrier, inc=1, device_id=in_column(lax.rem(z + d, n)), device_id_type=MESH)

    loop(1, rooms, greet_plane)
    loop(1, n, greet_column)
    pl.semaphore_wait(barrier, rooms - 1 + n - 1)

    def w1_copy(q):
        return remote(w_ref, wz.at[z], w1s.at[q], w1r.at[z], in_column(q))

    def w1_arrival(q):
        return remote(w_ref, wz.at[q], w1s.at[q], w1r.at[q], in_column(q))

    def ws_copy(q):
        return remote(w_ref, ws.at[g], wss.at[q], wsr.at[g], (q, f))

    def ws_arrival(q):
        return remote(w_ref, ws.at[q], wss.at[q], wsr.at[q], (q, f))

    loop(1, n, lambda d: w1_copy(lax.rem(z + d, n)).start())
    loop(1, n, lambda d: ws_copy(lax.rem(g + d, n)).start())
    wz[z] = w_ref[...]
    ws[g] = w_ref[...]

    wide = bins + 128
    coarse = window // 64
    lane = lax.broadcasted_iota(jnp.int32, (8, wide), 1)
    bin_idx = jnp.where(
        lane < bins, 2 * rb * ((lane % half) // rb) + rb * (lane // half) + lane % rb, 1
    )
    sub = lax.broadcasted_iota(jnp.int32, (8, wide), 0)

    def trig_rows(base, factor, first):
        angle = (((sub + first) * factor * bin_idx) & (window - 1)).astype(jnp.float32) * (
            2.0 * math.pi / window
        )
        trc[pl.ds(base, 8), :] = jnp.cos(angle)
        trs[pl.ds(base, 8), :] = jnp.sin(angle)

    loop(0, coarse // 8, lambda i: trig_rows(pl.multiple_of(8 * i, 8), 64, 8 * i))
    trig_rows(coarse, 8, 0)
    trig_rows(coarse + 8, 1, 0)

    def table_rows(a):
        ac, as_ = trc[pl.ds(a, 1), :], trs[pl.ds(a, 1), :]
        bc, bs = trc[coarse : coarse + 8, :], trs[coarse : coarse + 8, :]
        cc, cs_ = trc[coarse + 8 : coarse + 16, :], trs[coarse + 8 : coarse + 16, :]
        mid_c = ac * bc - as_ * bs
        mid_s = as_ * bc + ac * bs
        for b in range(0, 8, 2):
            real, imag = [], []
            for e in (b, b + 1):
                c1, s1 = mid_c[e : e + 1, :], mid_s[e : e + 1, :]
                cosines = c1 * cc - s1 * cs_
                sines = s1[:, :bins] * cc[:, :bins] + c1[:, :bins] * cs_[:, :bins]
                taper = 0.5 - 0.5 * cosines[:, bins:]
                taper = jnp.concatenate([taper] * (bins // 128), axis=1)
                real.append(taper * cosines[:, :bins])
                imag.append(-(taper * sines))
            here = pl.ds(pl.multiple_of(64 * a + 8 * b, 16), 16)
            tab[here, :bins] = jnp.concatenate(real, axis=0).astype(jnp.bfloat16)
            tab[here, bins:] = jnp.concatenate(imag, axis=0).astype(jnp.bfloat16)

    loop(0, coarse, table_rows)

    block = min(256, bins)

    def spectra_block(i):
        here = pl.ds(pl.multiple_of(i * block, block), block)
        there = pl.ds(pl.multiple_of(bins + i * block, block), block)
        frames = raw_ref[...]
        re = jnp.dot(frames, tab[:, here], preferred_element_type=jnp.float32)
        im = jnp.dot(frames, tab[:, there], preferred_element_type=jnp.float32)
        energy = jnp.log1p((re * re + im * im) / window)
        kept = (energy * live_ref[...]).reshape(rows // 8, 8, block)
        mean = jnp.sum(kept, axis=1, keepdims=True)
        centered = energy.reshape(rows // 8, 8, block) - mean
        c_own[:, here] = centered.reshape(rows, block).astype(jnp.bfloat16)

    loop(0, bins // block, spectra_block)

    pair_copy = remote(c_own, c_pair, xs.at[0], xr.at[0], pair)
    pair_copy.start()

    def w2_copy(src, q):
        return remote(wz.at[src], wr.at[g, h], w2s.at[q], w2r.at[me], in_plane(q))

    def w2_arrival(q):
        return remote(wz.at[0], wr.at[q // 2, lax.rem(q, 2)], w2s.at[q], w2r.at[q], in_plane(q))

    def w2_send(src):
        for side in range(2):
            q = 2 * src + side

            @pl.when(q != me)
            def _():
                w2_copy(src, q).start()

    def w2_forward(d):
        src = lax.rem(z + d, n)
        w1_arrival(src).wait_recv()
        w2_send(src)

    w2_send(z)
    loop(1, n, w2_forward)
    wr[g, h] = wz[g]

    width = cs.shape[1]
    place = (
        lax.broadcasted_iota(jnp.int32, (rooms * width, rows), 0) == srow_ref[...]
    ).astype(jnp.bfloat16)

    def place_block(i):
        here = pl.ds(pl.multiple_of(i * block, block), block)
        spread = jnp.dot(place, c_own[:, here], preferred_element_type=jnp.float32)
        cs[:, :, here] = spread.astype(jnp.bfloat16).reshape(rooms, width, block)

    loop(0, bins // block, place_block)

    def c1_copy(q):
        return remote(cs.at[q], cr.at[me], c1s.at[q], c1r.at[me], in_plane(q))

    def c1_arrival(q):
        return remote(cs.at[q], cr.at[q], c1s.at[q], c1r.at[q], in_plane(q))

    loop(1, rooms, lambda d: c1_copy(lax.rem(me + d, rooms)).start())
    cr[me] = cs[me]

    loop(1, rooms, lambda d: w2_arrival(lax.rem(me + d, rooms)).wait_recv())
    loop(1, n, lambda d: ws_arrival(lax.rem(g + d, n)).wait_recv())

    w_rows = jnp.concatenate([wr[k].reshape(2 * rb, -1) for k in range(n)], axis=1)
    w_cols = jnp.concatenate([ws[k] for k in range(n)], axis=1)
    gram = lax.dot_general(
        w_rows,
        jnp.concatenate([w_cols] * 4, axis=0),
        (((1,), (1,)), ((), ())),
        preferred_element_type=jnp.float32,
    )
    quarter = lax.broadcasted_iota(jnp.int32, (16, 128), 1) // rb
    piece = jnp.zeros((16, 128), jnp.float32)
    for q in range(4):
        piece = jnp.where(quarter == q, gram[16 * q : 16 * q + 16, :], piece)
    gp[...] = piece.astype(jnp.bfloat16)

    def g1_copy(q):
        return remote(gp, gz.at[z], g1s.at[q], g1r.at[z], in_column(q))

    def g1_arrival(q):
        return remote(gp, gz.at[q], g1s.at[q], g1r.at[q], in_column(q))

    loop(1, n, lambda d: g1_copy(lax.rem(z + d, n)).start())
    gz[z] = gp[...]

    scaled = (w_rows.astype(jnp.float32) * gain_ref[...]).astype(jnp.bfloat16)
    mc[...] = jnp.dot(scaled, head_ref[...], preferred_element_type=jnp.float32).astype(jnp.bfloat16)

    def m1_copy(q):
        return remote(mc, mz.at[z], m1s.at[q], m1r.at[z], in_column(q))

    def m1_arrival(q):
        return remote(mc, mz.at[q], m1s.at[q], m1r.at[q], in_column(q))

    loop(1, n, lambda d: m1_copy(lax.rem(z + d, n)).start())
    mz[z] = mc[...]

    loop(1, n, lambda d: g1_arrival(lax.rem(z + d, n)).wait_recv())
    for tile in range(n // 4):
        pieces = [gz[4 * tile + k].astype(jnp.float32) for k in range(4)]
        for q in range(4):
            strip = jnp.zeros((16, 128), jnp.float32)
            for k in range(4):
                shift = (rb * (k - q)) % 128
                moved = pltpu.roll(pieces[k], shift, 1) if shift else pieces[k]
                strip = jnp.where(quarter == k, moved, strip)
            gs[16 * q : 16 * q + 16, 128 * tile : 128 * tile + 128] = strip.astype(jnp.bfloat16)

    def g2_copy(q):
        return remote(gs, gf.at[g], g2s.at[q], g2r.at[g], (2 * (q // 2) + h, 2 * z + lax.rem(q, 2)))

    def g2_arrival(k):
        return remote(gs, gf.at[k], g2s.at[0], g2r.at[k], (k, 2 * z + core))

    own = 2 * (g // 2) + h

    def g2_each(act):
        def step(d):
            q = lax.rem(own + d, n)

            @pl.when((2 * (q // 2) + h != g) | (lax.rem(q, 2) != h))
            def _():
                act(g2_copy(q))

        return step

    loop(0, n, g2_each(lambda copy: copy.start()))

    @pl.when(h == core)
    def _():
        gf[g] = gs[...]

    def m2_copy(q):
        return remote(mz.at[q], mr.at[g], m2s.at[q], m2r.at[g], (q, f))

    def m2_arrival(q):
        return remote(mz.at[q], mr.at[q], m2s.at[q], m2r.at[q], (q, f))

    def m2_send(src):
        @pl.when(src != g)
        def _():
            m2_copy(src).start()

    def m2_forward(d):
        src = lax.rem(z + d, n)
        m1_arrival(src).wait_recv()
        m2_send(src)

    m2_send(z)
    loop(1, n, m2_forward)
    mr[g] = mz[g]

    pair_copy.wait_recv()

    def g2_wait(k):
        @pl.when((k != g) | (h != core))
        def _():
            g2_arrival(k).wait_recv()

    loop(0, n, g2_wait)
    mine = pl.ds(pl.multiple_of(core * half, half), half)
    gram_low = gf[:, :rb, :].reshape(half, half)
    gram_high = gf[:, rb:, :].reshape(half, half)

    def squares(frames):
        out = jnp.dot(frames[:, :half], gram_low, preferred_element_type=jnp.float32)
        out = out + jnp.dot(frames[:, half:], gram_high, preferred_element_type=jnp.float32)
        return jnp.sum(out * frames[:, mine].astype(jnp.float32), axis=1, keepdims=True)

    ms_send[...] = jnp.broadcast_to(squares(c_pair), ms_send.shape)
    ms_copy = remote(ms_send, ms_recv, xs.at[1], xr.at[1], pair)
    ms_copy.start()
    squares_here = squares(c_own)

    loop(1, rooms, lambda d: c1_arrival(lax.rem(me + d, rooms)).wait_recv())
    loop(1, n, lambda d: m2_arrival(lax.rem(g + d, n)).wait_recv())
    low = mr[:, :rb, :].reshape(half, -1)
    high = mr[:, rb:, :].reshape(half, -1)
    got = cr[...].reshape(rooms * width, bins)
    curves = jnp.dot(got[:, :half], low, preferred_element_type=jnp.float32)
    curves = curves + jnp.dot(got[:, half:], high, preferred_element_type=jnp.float32)
    y[...] = curves.astype(jnp.bfloat16).reshape(y.shape)

    def c3_copy(q):
        return remote(y.at[q], yr.at[me], c3s.at[q], c3r.at[me], in_plane(q))

    def c3_arrival(q):
        return remote(y.at[q], yr.at[q], c3s.at[q], c3r.at[q], in_plane(q))

    loop(1, rooms, lambda d: c3_copy(lax.rem(me + d, rooms)).start())
    yr[me] = y[me]

    loop(1, n, lambda d: w1_copy(lax.rem(z + d, n)).wait_send())
    loop(1, n, lambda d: ws_copy(lax.rem(g + d, n)).wait_send())
    loop(1, n, lambda d: g1_copy(lax.rem(z + d, n)).wait_send())
    loop(1, n, lambda d: m1_copy(lax.rem(z + d, n)).wait_send())
    loop(1, n, lambda d: m2_copy(lax.rem(g + d, n)).wait_send())
    loop(1, rooms, lambda d: w2_copy(0, lax.rem(me + d, rooms)).wait_send())
    loop(1, rooms, lambda d: c1_copy(lax.rem(me + d, rooms)).wait_send())
    loop(0, n, g2_each(lambda copy: copy.wait_send()))
    pair_copy.wait_send()

    ms_copy.wait()
    total = squares_here + ms_recv[:, :1]
    mean_square = jnp.maximum(total, 0.0) / head_ref.shape[0]
    scale = lax.rsqrt(mean_square + norm_epsilon)
    take = (
        lax.broadcasted_iota(jnp.int32, (rows, rooms * width), 1) == scol_ref[...]
    ).astype(jnp.bfloat16)
    loop(1, rooms, lambda d: c3_arrival(lax.rem(me + d, rooms)).wait_recv())
    back = jnp.dot(take, yr[...].reshape(rooms * width, -1), preferred_element_type=jnp.float32)
    out_ref[...] = (back * scale).astype(jnp.bfloat16)
    loop(1, rooms, lambda d: c3_copy(lax.rem(me + d, rooms)).wait_send())


def body(raw_clips, clip_lengths, clip_routes, w_spectral, norm_gain, room_heads):
    _, clip_count, slots, window = raw_clips.shape
    n = lax.axis_size("grp")
    rooms = lax.axis_size("fsdp")
    rows = clip_count * slots
    bins = window // 2
    rb, kc = w_spectral.shape
    curve = room_heads.shape[2]
    width = SLOTS * slots

    lengths = clip_lengths.reshape(clip_count)
    target = clip_routes.reshape(clip_count)
    clip_idx = jnp.arange(clip_count, dtype=jnp.int32)
    frame_idx = jnp.arange(slots, dtype=jnp.int32)
    same = (target[:, None] == target[None, :]) & (clip_idx[:, None] > clip_idx[None, :])
    slot = target * SLOTS + jnp.sum(same.astype(jnp.int32), axis=1)
    live = frame_idx[None, :] < lengths[:, None]
    slot_rows = jnp.where(live, slot[:, None] * slots + frame_idx[None, :], -1)
    weights = live.astype(jnp.float32) / lengths[:, None].astype(jnp.float32)

    bf16, f32 = jnp.bfloat16, jnp.float32
    vmem, sems = pltpu.VMEM, lambda k: pltpu.SemaphoreType.DMA((k,))
    coarse = window // 64
    out = pl.pallas_call(
        functools.partial(kernel, n),
        out_shape=jax.ShapeDtypeStruct((rows, curve), bf16),
        in_specs=[pl.BlockSpec(memory_space=pltpu.VMEM)] * 7,
        out_specs=pl.BlockSpec(memory_space=pltpu.VMEM),
        scratch_shapes=[
            vmem((window, 2 * bins), bf16),
            vmem((coarse + 16, bins + 128), f32),
            vmem((coarse + 16, bins + 128), f32),
            vmem((rows, bins), bf16),
            vmem((rows, bins), bf16),
            vmem((rooms, width, bins), bf16),
            vmem((rooms, width, bins), bf16),
            vmem((n, rb, kc), bf16),
            vmem((n, 2, rb, kc), bf16),
            vmem((n, rb, kc), bf16),
            vmem((2 * rb, curve), bf16),
            vmem((n, 2 * rb, curve), bf16),
            vmem((n, 2 * rb, curve), bf16),
            vmem((16, 128), bf16),
            vmem((n, 16, 128), bf16),
            vmem((2 * rb, bins // 2), bf16),
            vmem((n, 2 * rb, bins // 2), bf16),
            vmem((rooms, width, curve), bf16),
            vmem((rooms, width, curve), bf16),
            vmem((rows, 128), f32),
            vmem((rows, 128), f32),
            sems(n), sems(n), sems(n), sems(n),
            sems(rooms), sems(rooms),
            sems(n), sems(n), sems(n), sems(n),
            sems(n), sems(n), sems(n), sems(n),
            sems(rooms), sems(rooms), sems(rooms), sems(rooms),
            sems(2), sems(2),
        ],
        compiler_params=pltpu.CompilerParams(
            collective_id=0, has_side_effects=True, vmem_limit_bytes=56 * 2**20
        ),
    )(
        raw_clips.reshape(rows, window),
        w_spectral,
        norm_gain.reshape(1, -1),
        room_heads[0],
        slot_rows.reshape(1, rows),
        slot_rows.reshape(rows, 1),
        weights.reshape(rows, 1),
    )
    return out.reshape(1, clip_count, slots, curve)


def solution(mesh):
    return jax.shard_map(
        body,
        mesh=mesh,
        in_specs=(
            P("grp", "fsdp", None, None),
            P("grp", "fsdp", None),
            P("grp", "fsdp", None),
            P("fsdp", "grp"),
            P(),
            P("fsdp", None, None),
        ),
        out_specs=P("grp", "fsdp", None, None),
        check_vma=False,
    )
```

```python
import functools
import math

import jax
import jax.numpy as jnp
from jax import lax
from jax.experimental import pallas as pl
from jax.experimental.pallas import tpu as pltpu
from jax.sharding import PartitionSpec as P

SLOTS = 2
MESH = pl.DeviceIdType.MESH
norm_epsilon = 1e-05


def remote(src, dst, send_sem, recv_sem, device):
    return pltpu.make_async_remote_copy(
        src_ref=src,
        dst_ref=dst,
        send_sem=send_sem,
        recv_sem=recv_sem,
        device_id=device,
        device_id_type=MESH,
    )


def loop(low, high, step):
    def body(i, carry):
        step(i)
        return carry

    lax.fori_loop(low, high, body, 0)


def kernel(
    n,
    raw_ref, w_ref, gain_ref, head_ref, len_ref, route_ref,
    out_ref,
    tab, trc, trs, slot_col, slot_row, weight, c_own, c_pair, cs, cr, wz, wr, ws, mc, mz, mr,
    gp, gz, gs, gf, y, yr, ms_send, ms_recv,
    w1s, w1r, wss, wsr, w2s, w2r, m1s, m1r, m2s, m2r, g1s, g1r, g2s, g2r, c1s, c1r, c3s, c3r, xs, xr,
):
    rooms = 2 * n
    rows, window = raw_ref.shape
    bins = c_own.shape[1]
    half = bins // 2
    rb = w_ref.shape[0]
    g, f = lax.axis_index("grp"), lax.axis_index("fsdp")
    z, h = f // 2, lax.rem(f, 2)
    core = lax.rem(g, 2)
    me = 2 * g + h
    pair = (g + 1 - 2 * core, f)

    def in_plane(q):
        return (q // 2, 2 * z + lax.rem(q, 2))

    def in_column(q):
        return (g, 2 * q + h)

    barrier = pltpu.get_barrier_semaphore()

    def greet_plane(d):
        pl.semaphore_signal(barrier, inc=1, device_id=in_plane(lax.rem(me + d, rooms)), device_id_type=MESH)

    def greet_column(d):
        pl.semaphore_signal(barrier, inc=1, device_id=in_column(lax.rem(z + d, n)), device_id_type=MESH)

    back = lax.rem(z - g + 2 * n + 1, 4) - 1
    from_plane = lax.rem(z - back + n, n)

    def greet_senders(q):
        pl.semaphore_signal(barrier, inc=1, device_id=(q // 2, 2 * from_plane + lax.rem(q, 2)), device_id_type=MESH)

    @pl.when(back != 0)
    def _():
        loop(0, rooms, greet_senders)

    loop(1, rooms, greet_plane)
    loop(1, n, greet_column)
    pl.semaphore_wait(barrier, rooms - 1 + n - 1 + 3 * 4 * 2)

    far = (n // 2, n // 4, 3 * n // 4)

    def w1_copy(k):
        return remote(w_ref, wz.at[k], w1s.at[k], w1r.at[k], in_column(lax.rem(z + far[k], n)))

    def ws_copy(q):
        return remote(w_ref, ws.at[g], wss.at[q], wsr.at[g], (q, f))

    def ws_arrival(q):
        return remote(w_ref, ws.at[q], wss.at[q], wsr.at[q], (q, f))

    for k in range(3):
        w1_copy(k).start()

    near = (2, 1, n - 1, 0)

    def w2_each(k, act):
        src = w_ref if k == 3 else wz.at[k]
        origin = z if k == 3 else lax.rem(z + n - far[k], n)
        for e in range(4):
            for side in range(2):
                plane = lax.rem(z + near[e], n)
                copy = remote(
                    src, wr.at[g, h], w2s.at[8 * k + 2 * e + side], w2r.at[me], (origin, 2 * plane + side)
                )
                if e < 3:
                    act(copy)
                else:

                    @pl.when((origin != g) | (h != side))
                    def _():
                        act(copy)

    def w2_arrival(q):
        return remote(w_ref, wr.at[q // 2, lax.rem(q, 2)], w2s.at[0], w2r.at[q], in_plane(q))

    w2_each(3, lambda copy: copy.start())
    loop(1, n, lambda d: ws_copy(lax.rem(g + d, n)).start())
    ws[g] = w_ref[...]

    clips = len_ref.shape[1]
    row = lax.broadcasted_iota(jnp.int32, (rows, clips), 0)
    other = lax.broadcasted_iota(jnp.int32, (rows, clips), 1)
    lengths = jnp.broadcast_to(len_ref[...].astype(jnp.float32), (rows, clips))
    routes = jnp.broadcast_to(route_ref[...].astype(jnp.float32), (rows, clips))

    def total(kept, of):
        return jnp.sum(jnp.where(kept, of, 0.0), axis=1, keepdims=True)

    length = total(other == row // 8, lengths)
    route = total(other == row // 8, routes)
    rank = total((other < row // 8) & (routes == route), jnp.ones_like(routes))
    frame = (lax.broadcasted_iota(jnp.int32, (rows, 1), 0) % 8).astype(jnp.float32)
    slot = jnp.where(frame < length, (route * SLOTS + rank) * 8.0 + frame, -1.0)
    slot_all = jnp.broadcast_to(slot, (rows, 128))
    slot_col[...] = slot_all
    slot_row[...] = jnp.transpose(slot_all)[:8, :]
    weight[...] = jnp.broadcast_to(jnp.where(frame < length, 1.0 / length, 0.0), (rows, 128))

    wide = bins + 128
    coarse = window // 64
    lane = lax.broadcasted_iota(jnp.int32, (8, wide), 1)
    bin_idx = jnp.where(
        lane < bins, 2 * rb * ((lane % half) // rb) + rb * (lane // half) + lane % rb, 1
    )
    sub = lax.broadcasted_iota(jnp.int32, (8, wide), 0)

    def trig_rows(base, factor, first):
        angle = (((sub + first) * factor * bin_idx) & (window - 1)).astype(jnp.float32) * (
            2.0 * math.pi / window
        )
        trc[pl.ds(base, 8), :] = jnp.cos(angle)
        trs[pl.ds(base, 8), :] = jnp.sin(angle)

    loop(0, coarse // 8, lambda i: trig_rows(pl.multiple_of(8 * i, 8), 64, 8 * i))
    trig_rows(coarse, 8, 0)
    trig_rows(coarse + 8, 1, 0)

    def table_rows(a):
        ac, as_ = trc[pl.ds(a, 1), :], trs[pl.ds(a, 1), :]
        bc, bs = trc[coarse : coarse + 8, :], trs[coarse : coarse + 8, :]
        cc, cs_ = trc[coarse + 8 : coarse + 16, :], trs[coarse + 8 : coarse + 16, :]
        mid_c = ac * bc - as_ * bs
        mid_s = as_ * bc + ac * bs
        for b in range(0, 8, 2):
            real, imag = [], []
            for e in (b, b + 1):
                c1, s1 = mid_c[e : e + 1, :], mid_s[e : e + 1, :]
                cosines = c1 * cc - s1 * cs_
                sines = s1[:, :bins] * cc[:, :bins] + c1[:, :bins] * cs_[:, :bins]
                taper = 0.5 - 0.5 * cosines[:, bins:]
                taper = jnp.concatenate([taper] * (bins // 128), axis=1)
                real.append(taper * cosines[:, :bins])
                imag.append(-(taper * sines))
            here = pl.ds(pl.multiple_of(64 * a + 8 * b, 16), 16)
            tab[here, :bins] = jnp.concatenate(real, axis=0).astype(jnp.bfloat16)
            tab[here, bins:] = jnp.concatenate(imag, axis=0).astype(jnp.bfloat16)

    loop(0, coarse, table_rows)

    for k in range(3):
        w1_copy(k).wait_recv()
        w2_each(k, lambda copy: copy.start())

    @pl.when(back == 0)
    def _():
        for k in range(4):
            origin = z if k == 3 else lax.rem(z + n - far[k], n)

            @pl.when(origin == g)
            def _():
                wr[g, h] = w_ref[...] if k == 3 else wz[k]

    block = min(256, bins)

    def spectra_block(i):
        here = pl.ds(pl.multiple_of(i * block, block), block)
        there = pl.ds(pl.multiple_of(bins + i * block, block), block)
        frames = raw_ref[...]
        re = jnp.dot(frames, tab[:, here], preferred_element_type=jnp.float32)
        im = jnp.dot(frames, tab[:, there], preferred_element_type=jnp.float32)
        energy = jnp.log1p((re * re + im * im) / window)
        kept = (energy * weight[:, :1]).reshape(rows // 8, 8, block)
        mean = jnp.sum(kept, axis=1, keepdims=True)
        centered = energy.reshape(rows // 8, 8, block) - mean
        c_own[:, here] = centered.reshape(rows, block).astype(jnp.bfloat16)

    loop(0, bins // block, spectra_block)

    pair_copy = remote(c_own, c_pair, xs.at[0], xr.at[0], pair)
    pair_copy.start()

    width = cs.shape[1]
    place = (
        lax.broadcasted_iota(jnp.int32, (rooms * width, rows), 0).astype(jnp.float32)
        == slot_row[:1, :]
    ).astype(jnp.bfloat16)

    def place_block(i):
        here = pl.ds(pl.multiple_of(i * block, block), block)
        spread = jnp.dot(place, c_own[:, here], preferred_element_type=jnp.float32)
        cs[:, :, here] = spread.astype(jnp.bfloat16).reshape(rooms, width, block)

    loop(0, bins // block, place_block)

    def c1_copy(q):
        return remote(cs.at[q], cr.at[me], c1s.at[q], c1r.at[me], in_plane(q))

    def c1_arrival(q):
        return remote(cs.at[q], cr.at[q], c1s.at[q], c1r.at[q], in_plane(q))

    loop(1, rooms, lambda d: c1_copy(lax.rem(me + d, rooms)).start())
    cr[me] = cs[me]

    def w2_wait(q):
        @pl.when((q != me) | (back != 0))
        def _():
            w2_arrival(q).wait_recv()

    loop(0, rooms, w2_wait)
    loop(1, n, lambda d: ws_arrival(lax.rem(g + d, n)).wait_recv())

    w_rows = jnp.concatenate([wr[k].reshape(2 * rb, -1) for k in range(n)], axis=1)
    w_cols = jnp.concatenate([ws[k] for k in range(n)], axis=1)
    gram = lax.dot_general(
        w_rows,
        jnp.concatenate([w_cols] * 4, axis=0),
        (((1,), (1,)), ((), ())),
        preferred_element_type=jnp.float32,
    )
    quarter = lax.broadcasted_iota(jnp.int32, (16, 128), 1) // rb
    piece = jnp.zeros((16, 128), jnp.float32)
    for q in range(4):
        piece = jnp.where(quarter == q, gram[16 * q : 16 * q + 16, :], piece)
    gp[...] = piece.astype(jnp.bfloat16)

    def g1_copy(q):
        return remote(gp, gz.at[z], g1s.at[q], g1r.at[z], in_column(q))

    def g1_arrival(q):
        return remote(gp, gz.at[q], g1s.at[q], g1r.at[q], in_column(q))

    loop(1, n, lambda d: g1_copy(lax.rem(z + d, n)).start())
    gz[z] = gp[...]

    scaled = w_rows.astype(jnp.float32) * gain_ref[...]
    scaled_high = scaled.astype(jnp.bfloat16)
    scaled_low = (scaled - scaled_high.astype(jnp.float32)).astype(jnp.bfloat16)
    both = jnp.concatenate([scaled_high, scaled_low], axis=0)
    product = jnp.dot(both, head_ref[...], preferred_element_type=jnp.float32)
    mc[...] = (product[: 2 * rb] + product[2 * rb :]).astype(jnp.bfloat16)

    def m1_copy(k):
        return remote(mc, mz.at[k], m1s.at[k], m1r.at[k], in_column(lax.rem(z + far[k], n)))

    def m2_each(k, act):
        src = mc if k == 3 else mz.at[k]
        origin = z if k == 3 else lax.rem(z + n - far[k], n)
        for e in range(4):
            plane = lax.rem(z + near[e], n)
            copy = remote(src, mr.at[g], m2s.at[4 * k + e], m2r.at[g], (origin, 2 * plane + h))
            if e < 3:
                act(copy)
            else:

                @pl.when(origin != g)
                def _():
                    act(copy)

    def m2_arrival(q):
        return remote(mc, mr.at[q], m2s.at[0], m2r.at[q], (q, f))

    for k in range(3):
        m1_copy(k).start()
    m2_each(3, lambda copy: copy.start())
    for k in range(3):
        m1_copy(k).wait_recv()
        m2_each(k, lambda copy: copy.start())

    @pl.when(back == 0)
    def _():
        for k in range(4):
            origin = z if k == 3 else lax.rem(z + n - far[k], n)

            @pl.when(origin == g)
            def _():
                mr[g] = mc[...] if k == 3 else mz[k]

    loop(1, n, lambda d: g1_arrival(lax.rem(z + d, n)).wait_recv())
    for tile in range(n // 4):
        pieces = [gz[4 * tile + k].astype(jnp.float32) for k in range(4)]
        for q in range(4):
            strip = jnp.zeros((16, 128), jnp.float32)
            for k in range(4):
                shift = (rb * (k - q)) % 128
                moved = pltpu.roll(pieces[k], shift, 1) if shift else pieces[k]
                strip = jnp.where(quarter == k, moved, strip)
            gs[16 * q : 16 * q + 16, 128 * tile : 128 * tile + 128] = strip.astype(jnp.bfloat16)

    def g2_copy(q):
        return remote(gs, gf.at[g], g2s.at[q], g2r.at[g], (2 * (q // 2) + h, 2 * z + lax.rem(q, 2)))

    def g2_arrival(k):
        return remote(gs, gf.at[k], g2s.at[0], g2r.at[k], (k, 2 * z + core))

    own = 2 * (g // 2) + h

    def g2_each(act):
        def step(d):
            q = lax.rem(own + d, n)

            @pl.when((2 * (q // 2) + h != g) | (lax.rem(q, 2) != h))
            def _():
                act(g2_copy(q))

        return step

    loop(0, n, g2_each(lambda copy: copy.start()))

    @pl.when(h == core)
    def _():
        gf[g] = gs[...]

    loop(1, rooms, lambda d: c1_arrival(lax.rem(me + d, rooms)).wait_recv())
    def m2_wait(q):
        @pl.when((q != g) | (back != 0))
        def _():
            m2_arrival(q).wait_recv()

    loop(0, n, m2_wait)
    low = mr[:, :rb, :].reshape(half, -1)
    high = mr[:, rb:, :].reshape(half, -1)
    got = cr[...].reshape(rooms * width, bins)
    curves = jnp.dot(got[:, :half], low, preferred_element_type=jnp.float32)
    curves = curves + jnp.dot(got[:, half:], high, preferred_element_type=jnp.float32)
    y[...] = curves.astype(jnp.bfloat16).reshape(y.shape)

    def c3_copy(q):
        return remote(y.at[q], yr.at[me], c3s.at[q], c3r.at[me], in_plane(q))

    def c3_arrival(q):
        return remote(y.at[q], yr.at[q], c3s.at[q], c3r.at[q], in_plane(q))

    loop(1, rooms, lambda d: c3_copy(lax.rem(me + d, rooms)).start())
    yr[me] = y[me]

    pair_copy.wait_recv()

    def g2_wait(k):
        @pl.when((k != g) | (h != core))
        def _():
            g2_arrival(k).wait_recv()

    loop(0, n, g2_wait)
    mine = pl.ds(pl.multiple_of(core * half, half), half)
    gram_low = gf[:, :rb, :].reshape(half, half)
    gram_high = gf[:, rb:, :].reshape(half, half)

    def squares(frames):
        out = jnp.dot(frames[:, :half], gram_low, preferred_element_type=jnp.float32)
        out = out + jnp.dot(frames[:, half:], gram_high, preferred_element_type=jnp.float32)
        return jnp.sum(out * frames[:, mine].astype(jnp.float32), axis=1, keepdims=True)

    ms_send[...] = jnp.broadcast_to(squares(c_pair), ms_send.shape)
    ms_copy = remote(ms_send, ms_recv, xs.at[1], xr.at[1], pair)
    ms_copy.start()
    squares_here = squares(c_own)

    for k in range(3):
        w1_copy(k).wait_send()
        m1_copy(k).wait_send()
    for k in range(4):
        w2_each(k, lambda copy: copy.wait_send())
        m2_each(k, lambda copy: copy.wait_send())
    loop(1, n, lambda d: ws_copy(lax.rem(g + d, n)).wait_send())
    loop(1, n, lambda d: g1_copy(lax.rem(z + d, n)).wait_send())
    loop(1, rooms, lambda d: c1_copy(lax.rem(me + d, rooms)).wait_send())
    loop(0, n, g2_each(lambda copy: copy.wait_send()))
    pair_copy.wait_send()

    ms_copy.wait()
    square_sum = squares_here + ms_recv[:, :1]
    mean_square = jnp.maximum(square_sum, 0.0) / head_ref.shape[0]
    scale = lax.rsqrt(mean_square + norm_epsilon)
    take = (
        lax.broadcasted_iota(jnp.int32, (rows, rooms * width), 1).astype(jnp.float32)
        == slot_col[:, :1]
    ).astype(jnp.bfloat16)
    loop(1, rooms, lambda d: c3_arrival(lax.rem(me + d, rooms)).wait_recv())
    found = jnp.dot(take, yr[...].reshape(rooms * width, -1), preferred_element_type=jnp.float32)
    out_ref[...] = (found * scale).astype(jnp.bfloat16)
    loop(1, rooms, lambda d: c3_copy(lax.rem(me + d, rooms)).wait_send())


def body(raw_clips, clip_lengths, clip_routes, w_spectral, norm_gain, room_heads):
    _, clip_count, slots, window = raw_clips.shape
    n = lax.axis_size("grp")
    rooms = lax.axis_size("fsdp")
    rows = clip_count * slots
    bins = window // 2
    rb, kc = w_spectral.shape
    curve = room_heads.shape[2]
    width = SLOTS * slots

    bf16, f32 = jnp.bfloat16, jnp.float32
    vmem, sems = pltpu.VMEM, lambda k: pltpu.SemaphoreType.DMA((k,))
    coarse = window // 64
    out = pl.pallas_call(
        functools.partial(kernel, n),
        out_shape=jax.ShapeDtypeStruct((rows, curve), bf16),
        in_specs=[pl.BlockSpec(memory_space=pltpu.VMEM)] * 6,
        out_specs=pl.BlockSpec(memory_space=pltpu.VMEM),
        scratch_shapes=[
            vmem((window, 2 * bins), bf16),
            vmem((coarse + 16, bins + 128), f32),
            vmem((coarse + 16, bins + 128), f32),
            vmem((rows, 128), f32),
            vmem((8, rows), f32),
            vmem((rows, 128), f32),
            vmem((rows, bins), bf16),
            vmem((rows, bins), bf16),
            vmem((rooms, width, bins), bf16),
            vmem((rooms, width, bins), bf16),
            vmem((3, rb, kc), bf16),
            vmem((n, 2, rb, kc), bf16),
            vmem((n, rb, kc), bf16),
            vmem((2 * rb, curve), bf16),
            vmem((3, 2 * rb, curve), bf16),
            vmem((n, 2 * rb, curve), bf16),
            vmem((16, 128), bf16),
            vmem((n, 16, 128), bf16),
            vmem((2 * rb, bins // 2), bf16),
            vmem((n, 2 * rb, bins // 2), bf16),
            vmem((rooms, width, curve), bf16),
            vmem((rooms, width, curve), bf16),
            vmem((rows, 128), f32),
            vmem((rows, 128), f32),
            sems(3), sems(3), sems(n), sems(n),
            sems(rooms), sems(rooms),
            sems(3), sems(3), sems(16), sems(n),
            sems(n), sems(n), sems(n), sems(n),
            sems(rooms), sems(rooms), sems(rooms), sems(rooms),
            sems(2), sems(2),
        ],
        compiler_params=pltpu.CompilerParams(
            collective_id=0, has_side_effects=True, vmem_limit_bytes=56 * 2**20
        ),
    )(
        raw_clips.reshape(rows, window),
        w_spectral,
        norm_gain.reshape(1, -1),
        room_heads[0],
        clip_lengths.reshape(1, clip_count),
        clip_routes.reshape(1, clip_count),
    )
    return out.reshape(1, clip_count, slots, curve)


def solution(mesh):
    return jax.shard_map(
        body,
        mesh=mesh,
        in_specs=(
            P("grp", "fsdp", None, None),
            P("grp", "fsdp", None),
            P("grp", "fsdp", None),
            P("fsdp", "grp"),
            P(),
            P("fsdp", None, None),
        ),
        out_specs=P("grp", "fsdp", None, None),
        check_vma=False,
    )
```

```python
import functools
import math

import jax
import jax.numpy as jnp
from jax import lax
from jax.experimental import pallas as pl
from jax.experimental.pallas import tpu as pltpu
from jax.sharding import PartitionSpec as P

SLOTS = 2
MESH = pl.DeviceIdType.MESH
norm_epsilon = 1e-05


def remote(src, dst, send_sem, recv_sem, device):
    return pltpu.make_async_remote_copy(
        src_ref=src,
        dst_ref=dst,
        send_sem=send_sem,
        recv_sem=recv_sem,
        device_id=device,
        device_id_type=MESH,
    )


def loop(low, high, step):
    def body(i, carry):
        step(i)
        return carry

    lax.fori_loop(low, high, body, 0)


def kernel(
    n,
    raw_hbm, w_hbm, gain_hbm, head_hbm, len_hbm, route_hbm,
    out_ref,
    raw_ref, w_ref, gain_ref, head_ref, len_ref, route_ref, loads,
    tab, trc, trs, slot_col, slot_row, weight, c_own, c_pair, cs, cr, wz, wr, ws, mc, mz, mr,
    gp, gz, gs, gf, y, yr, ms_send, ms_own, ms_recv,
    w1s, w1r, wss, wsr, w2s, w2r, m1s, m1r, m2s, m2r, g1s, g1r, g2s, g2r, c1s, c1r, c3s, c3r, xs, xr,
):
    rooms = 2 * n
    rows, window = raw_ref.shape
    bins = c_own.shape[1]
    half = bins // 2
    rb = w_ref.shape[0]
    g, f = lax.axis_index("grp"), lax.axis_index("fsdp")
    z, h = f // 2, lax.rem(f, 2)
    core = lax.rem(g, 2)
    me = 2 * g + h
    pair = (g + 1 - 2 * core, f)

    def in_plane(q):
        return (q // 2, 2 * z + lax.rem(q, 2))

    def in_column(q):
        return (g, 2 * q + h)

    barrier = pltpu.get_barrier_semaphore()
    placed = ((w_hbm, w_ref), (len_hbm, len_ref), (route_hbm, route_ref), (raw_hbm, raw_ref), (head_hbm, head_ref), (gain_hbm, gain_ref))
    load = [pltpu.make_async_copy(src, dst, loads.at[k]) for k, (src, dst) in enumerate(placed)]
    load[0].start()

    def greet_plane(d):
        pl.semaphore_signal(barrier, inc=1, device_id=in_plane(lax.rem(me + d, rooms)), device_id_type=MESH)

    def greet_column(d):
        pl.semaphore_signal(barrier, inc=1, device_id=in_column(lax.rem(z + d, n)), device_id_type=MESH)

    back = lax.rem(z - g + 2 * n + 1, 4) - 1
    from_plane = lax.rem(z - back + 4 * lax.rem(g, 2) * ((back + 1) // 3) + n, n)

    def greet_senders(q):
        pl.semaphore_signal(barrier, inc=1, device_id=(q // 2, 2 * from_plane + lax.rem(q, 2)), device_id_type=MESH)

    @pl.when(back != 0)
    def _():
        loop(0, rooms, greet_senders)

    loop(1, rooms, greet_plane)
    loop(1, n, greet_column)
    for copy in load[1:]:
        copy.start()
    load[0].wait()
    pl.semaphore_wait(barrier, rooms - 1 + n - 1 + 3 * 4 * 2)

    far = (n // 2, n // 4, 3 * n // 4)

    def w1_copy(k):
        return remote(w_ref, wz.at[k], w1s.at[k], w1r.at[k], in_column(lax.rem(z + far[k], n)))

    def ws_copy(q):
        return remote(w_ref, ws.at[g], wss.at[q], wsr.at[g], (q, f))

    def ws_arrival(q):
        return remote(w_ref, ws.at[q], wss.at[q], wsr.at[q], (q, f))

    for k in range(3):
        w1_copy(k).start()

    near = (n + 2 - 4 * lax.rem(z, 2), 1, n - 1, 0)

    def w2_each(k, act):
        src = w_ref if k == 3 else wz.at[k]
        origin = z if k == 3 else lax.rem(z + n - far[k], n)
        for e in range(4):
            for side in range(2):
                plane = lax.rem(z + near[e], n)
                copy = remote(
                    src, wr.at[g, h], w2s.at[8 * k + 2 * e + side], w2r.at[me], (origin, 2 * plane + side)
                )
                if e < 3:
                    act(copy)
                else:

                    @pl.when((origin != g) | (h != side))
                    def _():
                        act(copy)

    def w2_arrival(q):
        return remote(w_ref, wr.at[q // 2, lax.rem(q, 2)], w2s.at[0], w2r.at[q], in_plane(q))

    w2_each(3, lambda copy: copy.start())
    loop(1, n, lambda d: ws_copy(lax.rem(g + d, n)).start())
    ws[g] = w_ref[...]

    load[1].wait()
    load[2].wait()

    clips = len_ref.shape[1]
    row = lax.broadcasted_iota(jnp.int32, (rows, clips), 0)
    other = lax.broadcasted_iota(jnp.int32, (rows, clips), 1)
    lengths = jnp.broadcast_to(len_ref[...].astype(jnp.float32), (rows, clips))
    routes = jnp.broadcast_to(route_ref[...].astype(jnp.float32), (rows, clips))

    def total(kept, of):
        return jnp.sum(jnp.where(kept, of, 0.0), axis=1, keepdims=True)

    length = total(other == row // 8, lengths)
    route = total(other == row // 8, routes)
    rank = total((other < row // 8) & (routes == route), jnp.ones_like(routes))
    frame = (lax.broadcasted_iota(jnp.int32, (rows, 1), 0) % 8).astype(jnp.float32)
    slot = jnp.where(frame < length, (route * SLOTS + rank) * 8.0 + frame, -1.0)
    slot_all = jnp.broadcast_to(slot, (rows, 128))
    slot_col[...] = slot_all
    slot_row[...] = jnp.transpose(slot_all)[:8, :]
    weight[...] = jnp.broadcast_to(jnp.where(frame < length, 1.0 / length, 0.0), (rows, 128))

    wide = bins + 128
    coarse = window // 64
    lane = lax.broadcasted_iota(jnp.int32, (8, wide), 1)
    bin_idx = jnp.where(
        lane < bins, 2 * rb * ((lane % half) // rb) + rb * (lane // half) + lane % rb, 1
    )
    sub = lax.broadcasted_iota(jnp.int32, (8, wide), 0)

    def trig_rows(base, factor, first):
        angle = (((sub + first) * factor * bin_idx) & (window - 1)).astype(jnp.float32) * (
            2.0 * math.pi / window
        )
        trc[pl.ds(base, 8), :] = jnp.cos(angle)
        trs[pl.ds(base, 8), :] = jnp.sin(angle)

    loop(0, coarse // 8, lambda i: trig_rows(pl.multiple_of(8 * i, 8), 64, 8 * i))
    trig_rows(coarse, 8, 0)
    trig_rows(coarse + 8, 1, 0)

    def table_rows(a):
        ac, as_ = trc[pl.ds(a, 1), :], trs[pl.ds(a, 1), :]
        bc, bs = trc[coarse : coarse + 8, :], trs[coarse : coarse + 8, :]
        cc, cs_ = trc[coarse + 8 : coarse + 16, :], trs[coarse + 8 : coarse + 16, :]
        mid_c = ac * bc - as_ * bs
        mid_s = as_ * bc + ac * bs
        for b in range(0, 8, 2):
            real, imag = [], []
            for e in (b, b + 1):
                c1, s1 = mid_c[e : e + 1, :], mid_s[e : e + 1, :]
                cosines = c1 * cc - s1 * cs_
                sines = s1[:, :bins] * cc[:, :bins] + c1[:, :bins] * cs_[:, :bins]
                taper = 0.5 - 0.5 * cosines[:, bins:]
                taper = jnp.concatenate([taper] * (bins // 128), axis=1)
                real.append(taper * cosines[:, :bins])
                imag.append(-(taper * sines))
            here = pl.ds(pl.multiple_of(64 * a + 8 * b, 16), 16)
            tab[here, :bins] = jnp.concatenate(real, axis=0).astype(jnp.bfloat16)
            tab[here, bins:] = jnp.concatenate(imag, axis=0).astype(jnp.bfloat16)

    loop(0, coarse, table_rows)

    for k in range(3):
        w1_copy(k).wait_recv()
        w2_each(k, lambda copy: copy.start())

    @pl.when(back == 0)
    def _():
        for k in range(4):
            origin = z if k == 3 else lax.rem(z + n - far[k], n)

            @pl.when(origin == g)
            def _():
                wr[g, h] = w_ref[...] if k == 3 else wz[k]

    block = min(256, bins)

    def spectra_block(i):
        here = pl.ds(pl.multiple_of(i * block, block), block)
        there = pl.ds(pl.multiple_of(bins + i * block, block), block)
        frames = raw_ref[...]
        re = jnp.dot(frames, tab[:, here], preferred_element_type=jnp.float32)
        im = jnp.dot(frames, tab[:, there], preferred_element_type=jnp.float32)
        energy = jnp.log1p((re * re + im * im) / window)
        kept = (energy * weight[:, :1]).reshape(rows // 8, 8, block)
        mean = jnp.sum(kept, axis=1, keepdims=True)
        centered = energy.reshape(rows // 8, 8, block) - mean
        c_own[:, here] = centered.reshape(rows, block).astype(jnp.bfloat16)

    load[3].wait()
    loop(0, bins // block, spectra_block)

    pair_copy = remote(c_own, c_pair, xs.at[0], xr.at[0], pair)
    pair_copy.start()

    width = cs.shape[1]
    place = (
        lax.broadcasted_iota(jnp.int32, (rooms * width, rows), 0).astype(jnp.float32)
        == slot_row[:1, :]
    ).astype(jnp.bfloat16)

    def place_block(i):
        here = pl.ds(pl.multiple_of(i * block, block), block)
        spread = jnp.dot(place, c_own[:, here], preferred_element_type=jnp.float32)
        cs[:, :, here] = spread.astype(jnp.bfloat16).reshape(rooms, width, block)

    loop(0, bins // block, place_block)

    def c1_copy(q):
        return remote(cs.at[q], cr.at[me], c1s.at[0], c1r.at[0], in_plane(q))

    others = pl.ds(0, rooms - 1)
    c1_all = remote(cs.at[others], cr.at[others], c1s.at[0], c1r.at[0], pair)
    loop(1, rooms, lambda d: c1_copy(lax.rem(me + d, rooms)).start())
    cr[me] = cs[me]

    def w2_wait(q):
        @pl.when((q != me) | (back != 0))
        def _():
            w2_arrival(q).wait_recv()

    loop(0, rooms, w2_wait)
    loop(1, n, lambda d: ws_arrival(lax.rem(g + d, n)).wait_recv())

    w_rows = jnp.concatenate([wr[k].reshape(2 * rb, -1) for k in range(n)], axis=1)
    load[4].wait()
    load[5].wait()
    scaled = w_rows.astype(jnp.float32) * gain_ref[...]
    scaled_high = scaled.astype(jnp.bfloat16)
    scaled_low = (scaled - scaled_high.astype(jnp.float32)).astype(jnp.bfloat16)
    both = jnp.concatenate([scaled_high, scaled_low], axis=0)
    product = jnp.dot(both, head_ref[...], preferred_element_type=jnp.float32)
    mc[...] = (product[: 2 * rb] + product[2 * rb :]).astype(jnp.bfloat16)

    def m1_copy(k):
        return remote(mc, mz.at[k], m1s.at[k], m1r.at[k], in_column(lax.rem(z + far[k], n)))

    def m2_each(k, act):
        src = mc if k == 3 else mz.at[k]
        origin = z if k == 3 else lax.rem(z + n - far[k], n)
        for e in range(4):
            plane = lax.rem(z + near[e], n)
            copy = remote(src, mr.at[g], m2s.at[4 * k + e], m2r.at[g], (origin, 2 * plane + h))
            if e < 3:
                act(copy)
            else:

                @pl.when(origin != g)
                def _():
                    act(copy)

    def m2_arrival(q):
        return remote(mc, mr.at[q], m2s.at[0], m2r.at[q], (q, f))

    for k in range(3):
        m1_copy(k).start()
    m2_each(3, lambda copy: copy.start())
    w_cols = jnp.concatenate([ws[k] for k in range(n)], axis=1)
    gram = lax.dot_general(
        w_rows,
        jnp.concatenate([w_cols] * 4, axis=0),
        (((1,), (1,)), ((), ())),
        preferred_element_type=jnp.float32,
    )
    quarter = lax.broadcasted_iota(jnp.int32, (16, 128), 1) // rb
    piece = jnp.zeros((16, 128), jnp.float32)
    for q in range(4):
        piece = jnp.where(quarter == q, gram[16 * q : 16 * q + 16, :], piece)
    shift = lax.rem(z - g + n, n)
    twice = jnp.where((shift > 0) & (shift < n // 2), 2.0, 1.0)
    gp[...] = (piece * twice).astype(jnp.bfloat16)

    def g1_copy(q):
        return remote(gp, gz.at[shift], g1s.at[q], g1r.at[shift], in_column(q))

    def g1_arrival(k):
        return remote(gp, gz.at[k], g1s.at[0], g1r.at[k], in_column(lax.rem(g + k, n)))

    @pl.when(shift <= n // 2)
    def _():
        loop(1, n, lambda d: g1_copy(lax.rem(z + d, n)).start())
        gz[shift] = gp[...]

    for k in range(3):
        m1_copy(k).wait_recv()
        m2_each(k, lambda copy: copy.start())

    @pl.when(back == 0)
    def _():
        for k in range(4):
            origin = z if k == 3 else lax.rem(z + n - far[k], n)

            @pl.when(origin == g)
            def _():
                mr[g] = mc[...] if k == 3 else mz[k]

    def g1_wait(k):
        @pl.when(k != shift)
        def _():
            g1_arrival(k).wait_recv()

    loop(0, n // 2 + 1, g1_wait)

    def g2_copy(q):
        return remote(gz, gf.at[g], g2s.at[q], g2r.at[g], (2 * (q // 2) + h, 2 * z + lax.rem(q, 2)))

    def g2_arrival(k):
        return remote(gz, gf.at[k], g2s.at[0], g2r.at[k], (k, 2 * z + core))

    own = 2 * (g // 2) + h

    def g2_each(act):
        def step(d):
            q = lax.rem(own + d, n)

            @pl.when((2 * (q // 2) + h != g) | (lax.rem(q, 2) != h))
            def _():
                act(g2_copy(q))

        return step

    loop(0, n, g2_each(lambda copy: copy.start()))

    @pl.when(h == core)
    def _():
        gf[g] = gz[...]

    c1_all.wait_recv()
    def m2_wait(q):
        @pl.when((q != g) | (back != 0))
        def _():
            m2_arrival(q).wait_recv()

    loop(0, n, m2_wait)
    low = mr[:, :rb, :].reshape(half, -1)
    high = mr[:, rb:, :].reshape(half, -1)
    got = cr[...].reshape(rooms * width, bins)
    curves = jnp.dot(got[:, :half], low, preferred_element_type=jnp.float32)
    curves = curves + jnp.dot(got[:, half:], high, preferred_element_type=jnp.float32)
    y[...] = curves.astype(jnp.bfloat16).reshape(y.shape)

    def c3_copy(q):
        return remote(y.at[q], yr.at[me], c3s.at[0], c3r.at[0], in_plane(q))

    c3_all = remote(y.at[others], yr.at[others], c3s.at[0], c3r.at[0], pair)
    loop(1, rooms, lambda d: c3_copy(lax.rem(me + d, rooms)).start())
    yr[me] = y[me]

    pair_copy.wait_recv()

    def g2_wait(k):
        @pl.when((k != g) | (h != core))
        def _():
            g2_arrival(k).wait_recv()

    loop(0, n, g2_wait)
    def squares_of_group(m):
        for r in range(4):
            for q in range(4):
                pieces = [gf[4 * m + r, k].astype(jnp.float32) for k in range(n // 2 + 1)]
                for tile in range(3):
                    strip = jnp.zeros((16, 128), jnp.float32)
                    for k in range(4):
                        s = 4 * tile + k - r
                        if 0 <= s <= n // 2:
                            turn = (rb * (k - q)) % 128
                            moved = pltpu.roll(pieces[s], turn, 1) if turn else pieces[s]
                            strip = jnp.where(quarter == k, moved, strip)
                    low = 128 * (q // 2) + rb * r + 16 * (q % 2)
                    gs[low : low + 16, 128 * tile : 128 * tile + 128] = strip.astype(jnp.bfloat16)
        wide_low = pl.ds(pl.multiple_of(128 * m, 128), 128)
        wide_high = pl.ds(pl.multiple_of(half + 128 * m, 128), 128)
        for frames, sums in ((c_pair, ms_send), (c_own, ms_own)):
            part = jnp.concatenate([frames[:, wide_low], frames[:, wide_high]], axis=1)
            out = jnp.dot(part, gs[...], preferred_element_type=jnp.float32)
            for tile in range(3):
                cols = pl.ds(pl.multiple_of(core * half + 128 * lax.rem(m + tile, n // 4), 128), 128)
                sums[...] += out[:, 128 * tile : 128 * tile + 128] * frames[:, cols].astype(jnp.float32)

    ms_send[...] = jnp.zeros_like(ms_send)
    ms_own[...] = jnp.zeros_like(ms_own)
    loop(0, n // 4, squares_of_group)
    ms_copy = remote(ms_send, ms_recv, xs.at[1], xr.at[1], pair)
    ms_copy.start()

    for k in range(3):
        w1_copy(k).wait_send()
        m1_copy(k).wait_send()
    for k in range(4):
        w2_each(k, lambda copy: copy.wait_send())
        m2_each(k, lambda copy: copy.wait_send())
    loop(1, n, lambda d: ws_copy(lax.rem(g + d, n)).wait_send())

    @pl.when(shift <= n // 2)
    def _():
        loop(1, n, lambda d: g1_copy(lax.rem(z + d, n)).wait_send())

    c1_all.wait_send()
    loop(0, n, g2_each(lambda copy: copy.wait_send()))
    pair_copy.wait_send()

    ms_copy.wait()
    square_sum = jnp.sum(ms_own[...] + ms_recv[...], axis=1, keepdims=True)
    mean_square = jnp.maximum(square_sum, 0.0) / head_ref.shape[0]
    scale = lax.rsqrt(mean_square + norm_epsilon)
    take = (
        lax.broadcasted_iota(jnp.int32, (rows, rooms * width), 1).astype(jnp.float32)
        == slot_col[:, :1]
    ).astype(jnp.bfloat16)
    c3_all.wait_recv()
    found = jnp.dot(take, yr[...].reshape(rooms * width, -1), preferred_element_type=jnp.float32)
    out_ref[...] = (found * scale).astype(jnp.bfloat16)
    c3_all.wait_send()


def body(raw_clips, clip_lengths, clip_routes, w_spectral, norm_gain, room_heads):
    _, clip_count, slots, window = raw_clips.shape
    n = lax.axis_size("grp")
    rooms = lax.axis_size("fsdp")
    rows = clip_count * slots
    bins = window // 2
    rb, kc = w_spectral.shape
    curve = room_heads.shape[2]
    width = SLOTS * slots

    bf16, f32 = jnp.bfloat16, jnp.float32
    vmem, sems = pltpu.VMEM, lambda k: pltpu.SemaphoreType.DMA((k,))
    coarse = window // 64
    operands = (
        raw_clips.reshape(rows, window),
        w_spectral,
        norm_gain.reshape(1, -1),
        room_heads[0],
        clip_lengths.reshape(1, clip_count),
        clip_routes.reshape(1, clip_count),
    )
    out = pl.pallas_call(
        functools.partial(kernel, n),
        out_shape=jax.ShapeDtypeStruct((rows, curve), bf16),
        in_specs=[pl.BlockSpec(memory_space=pltpu.HBM)] * 6,
        out_specs=pl.BlockSpec(memory_space=pltpu.VMEM),
        scratch_shapes=[
            vmem((rows, window), bf16),
            vmem((rb, kc), bf16),
            vmem((1, n * kc), f32),
            vmem((n * kc, curve), bf16),
            vmem((1, clip_count), jnp.int32),
            vmem((1, clip_count), jnp.int32),
            sems(6),
            vmem((window, 2 * bins), bf16),
            vmem((coarse + 16, bins + 128), f32),
            vmem((coarse + 16, bins + 128), f32),
            vmem((rows, 128), f32),
            vmem((8, rows), f32),
            vmem((rows, 128), f32),
            vmem((rows, bins), bf16),
            vmem((rows, bins), bf16),
            vmem((rooms, width, bins), bf16),
            vmem((rooms, width, bins), bf16),
            vmem((3, rb, kc), bf16),
            vmem((n, 2, rb, kc), bf16),
            vmem((n, rb, kc), bf16),
            vmem((2 * rb, curve), bf16),
            vmem((3, 2 * rb, curve), bf16),
            vmem((n, 2 * rb, curve), bf16),
            vmem((16, 128), bf16),
            vmem((n // 2 + 1, 16, 128), bf16),
            vmem((256, 384), bf16),
            vmem((n, n // 2 + 1, 16, 128), bf16),
            vmem((rooms, width, curve), bf16),
            vmem((rooms, width, curve), bf16),
            vmem((rows, 128), f32),
            vmem((rows, 128), f32),
            vmem((rows, 128), f32),
            sems(3), sems(3), sems(n), sems(n),
            sems(rooms), sems(rooms),
            sems(3), sems(3), sems(16), sems(n),
            sems(n), sems(n), sems(n), sems(n),
            sems(1), sems(1), sems(1), sems(1),
            sems(2), sems(2),
        ],
        compiler_params=pltpu.CompilerParams(
            collective_id=0, has_side_effects=True, vmem_limit_bytes=32 * 2**20
        ),
    )(
        *(pltpu.with_memory_space_constraint(x, pltpu.HBM) for x in operands)
    )
    return out.reshape(1, clip_count, slots, curve)


def solution(mesh):
    return jax.shard_map(
        body,
        mesh=mesh,
        in_specs=(
            P("grp", "fsdp", None, None),
            P("grp", "fsdp", None),
            P("grp", "fsdp", None),
            P("fsdp", "grp"),
            P(),
            P("fsdp", None, None),
        ),
        out_specs=P("grp", "fsdp", None, None),
        check_vma=False,
    )
```

```python
import functools
import math

import jax
import jax.numpy as jnp
from jax import lax
from jax.experimental import pallas as pl
from jax.experimental.pallas import tpu as pltpu
from jax.sharding import PartitionSpec as P

SLOTS = 2
MESH = pl.DeviceIdType.MESH
norm_epsilon = 1e-05


def remote(src, dst, send_sem, recv_sem, device):
    return pltpu.make_async_remote_copy(
        src_ref=src,
        dst_ref=dst,
        send_sem=send_sem,
        recv_sem=recv_sem,
        device_id=device,
        device_id_type=MESH,
    )


def loop(low, high, step):
    def body(i, carry):
        step(i)
        return carry

    lax.fori_loop(low, high, body, 0)


def kernel(
    n,
    raw_hbm, w_hbm, gain_hbm, head_hbm, len_hbm, route_hbm,
    out_ref,
    raw_ref, w_ref, gain_ref, head_ref, len_ref, route_ref, loads,
    tab, trc, trs, slot_col, slot_row, weight, c_own, c_pair, cs, cr, wz, wr, ws, mc, mz, mr,
    gp, gz, gs, gf, y, yr, ms_send, ms_own, ms_recv,
    w1s, w1r, wss, wsr, w2s, w2r, m1s, m1r, m2s, m2r, g1s, g1r, g2s, g2r, c1s, c1r, c3s, c3r, xs, xr,
):
    rooms = 2 * n
    rows, window = raw_ref.shape
    bins = c_own.shape[1]
    half = bins // 2
    rb = w_ref.shape[0]
    g, f = lax.axis_index("grp"), lax.axis_index("fsdp")
    z, h = f // 2, lax.rem(f, 2)
    core = lax.rem(g, 2)
    me = 2 * g + h
    pair = (g + 1 - 2 * core, f)

    def in_plane(q):
        return (q // 2, 2 * z + lax.rem(q, 2))

    def in_column(q):
        return (g, 2 * q + h)

    barrier = pltpu.get_barrier_semaphore()
    placed = ((w_hbm, w_ref), (len_hbm, len_ref), (route_hbm, route_ref), (raw_hbm, raw_ref), (head_hbm, head_ref), (gain_hbm, gain_ref))
    load = [pltpu.make_async_copy(src, dst, loads.at[k]) for k, (src, dst) in enumerate(placed)]
    load[0].start()

    def greet_plane(d):
        pl.semaphore_signal(barrier, inc=1, device_id=in_plane(lax.rem(me + d, rooms)), device_id_type=MESH)

    def greet_column(d):
        pl.semaphore_signal(barrier, inc=1, device_id=in_column(lax.rem(z + d, n)), device_id_type=MESH)

    back = lax.rem(z - g + 2 * n + 1, 4) - 1
    from_plane = lax.rem(z - back + 4 * lax.rem(g, 2) * ((back + 1) // 3) + n, n)

    def greet_senders(q):
        pl.semaphore_signal(barrier, inc=1, device_id=(q // 2, 2 * from_plane + lax.rem(q, 2)), device_id_type=MESH)

    loop(1, n, greet_column)

    @pl.when(back != 0)
    def _():
        loop(0, rooms, greet_senders)

    loop(1, rooms, greet_plane)
    for copy in load[1:]:
        copy.start()
    load[0].wait()
    pl.semaphore_wait(barrier, rooms - 1 + n - 1 + 3 * 4 * 2)

    far = (n // 2, n // 4, 3 * n // 4)

    def w1_copy(k):
        return remote(w_ref, wz.at[k], w1s.at[k], w1r.at[k], in_column(lax.rem(z + far[k], n)))

    def ws_copy(q):
        return remote(w_ref, ws.at[g], wss.at[q], wsr.at[g], (q, f))

    def ws_arrival(q):
        return remote(w_ref, ws.at[q], wss.at[q], wsr.at[q], (q, f))

    for k in range(3):
        w1_copy(k).start()

    near = (n + 2 - 4 * lax.rem(z, 2), 1, n - 1, 0)

    def w2_each(k, act):
        src = w_ref if k == 3 else wz.at[k]
        origin = z if k == 3 else lax.rem(z + n - far[k], n)
        for e in range(4):
            for side in range(2):
                plane = lax.rem(z + near[e], n)
                copy = remote(
                    src, wr.at[g, h], w2s.at[8 * k + 2 * e + side], w2r.at[me], (origin, 2 * plane + side)
                )
                if e < 3:
                    act(copy)
                else:

                    @pl.when((origin != g) | (h != side))
                    def _():
                        act(copy)

    def w2_arrival(q):
        return remote(w_ref, wr.at[q // 2, lax.rem(q, 2)], w2s.at[0], w2r.at[q], in_plane(q))

    w2_each(3, lambda copy: copy.start())
    loop(1, n, lambda d: ws_copy(lax.rem(g + d, n)).start())
    ws[g] = w_ref[...]

    load[1].wait()
    load[2].wait()

    clips = len_ref.shape[1]
    row = lax.broadcasted_iota(jnp.int32, (rows, clips), 0)
    other = lax.broadcasted_iota(jnp.int32, (rows, clips), 1)
    lengths = jnp.broadcast_to(len_ref[...].astype(jnp.float32), (rows, clips))
    routes = jnp.broadcast_to(route_ref[...].astype(jnp.float32), (rows, clips))

    def total(kept, of):
        return jnp.sum(jnp.where(kept, of, 0.0), axis=1, keepdims=True)

    length = total(other == row // 8, lengths)
    route = total(other == row // 8, routes)
    rank = total((other < row // 8) & (routes == route), jnp.ones_like(routes))
    frame = (lax.broadcasted_iota(jnp.int32, (rows, 1), 0) % 8).astype(jnp.float32)
    slot = jnp.where(frame < length, (route * SLOTS + rank) * 8.0 + frame, -1.0)
    slot_all = jnp.broadcast_to(slot, (rows, 128))
    slot_col[...] = slot_all
    slot_row[...] = jnp.transpose(slot_all)[:8, :]
    weight[...] = jnp.broadcast_to(jnp.where(frame < length, 1.0 / length, 0.0), (rows, 128))

    wide = bins + 128
    coarse = window // 64
    lane = lax.broadcasted_iota(jnp.int32, (8, wide), 1)
    bin_idx = jnp.where(
        lane < bins, 2 * rb * ((lane % half) // rb) + rb * (lane // half) + lane % rb, 1
    )
    sub = lax.broadcasted_iota(jnp.int32, (8, wide), 0)

    def trig_rows(base, factor, first):
        angle = (((sub + first) * factor * bin_idx) & (window - 1)).astype(jnp.float32) * (
            2.0 * math.pi / window
        )
        trc[pl.ds(base, 8), :] = jnp.cos(angle)
        trs[pl.ds(base, 8), :] = jnp.sin(angle)

    loop(0, coarse // 8, lambda i: trig_rows(pl.multiple_of(8 * i, 8), 64, 8 * i))
    trig_rows(coarse, 8, 0)
    trig_rows(coarse + 8, 1, 0)

    def table_rows(a):
        ac, as_ = trc[pl.ds(a, 1), :], trs[pl.ds(a, 1), :]
        bc, bs = trc[coarse : coarse + 8, :], trs[coarse : coarse + 8, :]
        cc, cs_ = trc[coarse + 8 : coarse + 16, :], trs[coarse + 8 : coarse + 16, :]
        mid_c = ac * bc - as_ * bs
        mid_s = as_ * bc + ac * bs
        for b in range(0, 8, 2):
            real, imag = [], []
            for e in (b, b + 1):
                c1, s1 = mid_c[e : e + 1, :], mid_s[e : e + 1, :]
                cosines = c1 * cc - s1 * cs_
                sines = s1[:, :bins] * cc[:, :bins] + c1[:, :bins] * cs_[:, :bins]
                taper = 0.5 - 0.5 * cosines[:, bins:]
                taper = jnp.concatenate([taper] * (bins // 128), axis=1)
                real.append(taper * cosines[:, :bins])
                imag.append(-(taper * sines))
            here = pl.ds(pl.multiple_of(64 * a + 8 * b, 16), 16)
            tab[here, :bins] = jnp.concatenate(real, axis=0).astype(jnp.bfloat16)
            tab[here, bins:] = jnp.concatenate(imag, axis=0).astype(jnp.bfloat16)

    loop(0, coarse, table_rows)

    for k in range(3):
        w1_copy(k).wait_recv()
        w2_each(k, lambda copy: copy.start())

    @pl.when(back == 0)
    def _():
        for k in range(4):
            origin = z if k == 3 else lax.rem(z + n - far[k], n)

            @pl.when(origin == g)
            def _():
                wr[g, h] = w_ref[...] if k == 3 else wz[k]

    block = min(256, bins)

    def spectra_block(i):
        here = pl.ds(pl.multiple_of(i * block, block), block)
        there = pl.ds(pl.multiple_of(bins + i * block, block), block)
        frames = raw_ref[...]
        re = jnp.dot(frames, tab[:, here], preferred_element_type=jnp.float32)
        im = jnp.dot(frames, tab[:, there], preferred_element_type=jnp.float32)
        energy = jnp.log1p((re * re + im * im) / window)
        kept = (energy * weight[:, :1]).reshape(rows // 8, 8, block)
        mean = jnp.sum(kept, axis=1, keepdims=True)
        centered = energy.reshape(rows // 8, 8, block) - mean
        c_own[:, here] = centered.reshape(rows, block).astype(jnp.bfloat16)

    load[3].wait()
    loop(0, bins // block, spectra_block)

    pair_copy = remote(c_own, c_pair, xs.at[0], xr.at[0], pair)
    pair_copy.start()

    width = cs.shape[1]
    place = (
        lax.broadcasted_iota(jnp.int32, (rooms * width, rows), 0).astype(jnp.float32)
        == slot_row[:1, :]
    ).astype(jnp.bfloat16)

    def place_block(i):
        here = pl.ds(pl.multiple_of(i * block, block), block)
        spread = jnp.dot(place, c_own[:, here], preferred_element_type=jnp.float32)
        cs[:, :, here] = spread.astype(jnp.bfloat16).reshape(rooms, width, block)

    loop(0, bins // block, place_block)

    def c1_copy(q):
        return remote(cs.at[q], cr.at[me], c1s.at[0], c1r.at[0], in_plane(q))

    others = pl.ds(0, rooms - 1)
    c1_all = remote(cs.at[others], cr.at[others], c1s.at[0], c1r.at[0], pair)
    loop(1, rooms, lambda d: c1_copy(lax.rem(me + d, rooms)).start())
    cr[me] = cs[me]

    def w2_wait(q):
        @pl.when((q != me) | (back != 0))
        def _():
            w2_arrival(q).wait_recv()

    loop(0, rooms, w2_wait)
    loop(1, n, lambda d: ws_arrival(lax.rem(g + d, n)).wait_recv())

    w_rows = jnp.concatenate([wr[k].reshape(2 * rb, -1) for k in range(n)], axis=1)
    load[4].wait()
    load[5].wait()
    scaled = w_rows.astype(jnp.float32) * gain_ref[...]
    scaled_high = scaled.astype(jnp.bfloat16)
    scaled_low = (scaled - scaled_high.astype(jnp.float32)).astype(jnp.bfloat16)
    both = jnp.concatenate([scaled_high, scaled_low], axis=0)
    product = jnp.dot(both, head_ref[...], preferred_element_type=jnp.float32)
    mc[...] = (product[: 2 * rb] + product[2 * rb :]).astype(jnp.bfloat16)

    def m1_copy(k):
        return remote(mc, mz.at[k], m1s.at[k], m1r.at[k], in_column(lax.rem(z + far[k], n)))

    def m2_each(k, act):
        src = mc if k == 3 else mz.at[k]
        origin = z if k == 3 else lax.rem(z + n - far[k], n)
        for e in range(4):
            plane = lax.rem(z + near[e], n)
            copy = remote(src, mr.at[g], m2s.at[4 * k + e], m2r.at[g], (origin, 2 * plane + h))
            if e < 3:
                act(copy)
            else:

                @pl.when(origin != g)
                def _():
                    act(copy)

    def m2_arrival(q):
        return remote(mc, mr.at[q], m2s.at[0], m2r.at[q], (q, f))

    for k in range(3):
        m1_copy(k).start()
    m2_each(3, lambda copy: copy.start())
    w_cols = jnp.concatenate([ws[k] for k in range(n)], axis=1)
    gram = lax.dot_general(
        w_rows,
        jnp.concatenate([w_cols] * 4, axis=0),
        (((1,), (1,)), ((), ())),
        preferred_element_type=jnp.float32,
    )
    quarter = lax.broadcasted_iota(jnp.int32, (16, 128), 1) // rb
    piece = jnp.zeros((16, 128), jnp.float32)
    for q in range(4):
        piece = jnp.where(quarter == q, gram[16 * q : 16 * q + 16, :], piece)
    shift = lax.rem(z - g + n, n)
    twice = jnp.where((shift > 0) & (shift < n // 2), 2.0, 1.0)
    gp[...] = (piece * twice).astype(jnp.bfloat16)

    def g1_copy(q):
        return remote(gp, gz.at[shift], g1s.at[q], g1r.at[shift], in_column(q))

    def g1_arrival(k):
        return remote(gp, gz.at[k], g1s.at[0], g1r.at[k], in_column(lax.rem(g + k, n)))

    @pl.when(shift <= n // 2)
    def _():
        loop(1, n, lambda d: g1_copy(lax.rem(z + d, n)).start())
        gz[shift] = gp[...]

    for k in range(3):
        m1_copy(k).wait_recv()
        m2_each(k, lambda copy: copy.start())

    @pl.when(back == 0)
    def _():
        for k in range(4):
            origin = z if k == 3 else lax.rem(z + n - far[k], n)

            @pl.when(origin == g)
            def _():
                mr[g] = mc[...] if k == 3 else mz[k]

    def g1_wait(k):
        @pl.when(k != shift)
        def _():
            g1_arrival(k).wait_recv()

    loop(0, n // 2 + 1, g1_wait)

    def g2_copy(q):
        return remote(gz, gf.at[g], g2s.at[q], g2r.at[g], (2 * (q // 2) + h, 2 * z + lax.rem(q, 2)))

    def g2_arrival(k):
        return remote(gz, gf.at[k], g2s.at[0], g2r.at[k], (k, 2 * z + core))

    own = 2 * (g // 2) + h

    def g2_each(act):
        def step(d):
            q = lax.rem(own + d, n)

            @pl.when((2 * (q // 2) + h != g) | (lax.rem(q, 2) != h))
            def _():
                act(g2_copy(q))

        return step

    loop(0, n, g2_each(lambda copy: copy.start()))

    @pl.when(h == core)
    def _():
        gf[g] = gz[...]

    c1_all.wait_recv()
    def m2_wait(q):
        @pl.when((q != g) | (back != 0))
        def _():
            m2_arrival(q).wait_recv()

    loop(0, n, m2_wait)
    low = mr[:, :rb, :].reshape(half, -1)
    high = mr[:, rb:, :].reshape(half, -1)
    got = cr[...].reshape(rooms * width, bins)
    curves = jnp.dot(got[:, :half], low, preferred_element_type=jnp.float32)
    curves = curves + jnp.dot(got[:, half:], high, preferred_element_type=jnp.float32)
    y[...] = curves.astype(jnp.bfloat16).reshape(y.shape)

    def c3_copy(q):
        return remote(y.at[q], yr.at[me], c3s.at[0], c3r.at[0], in_plane(q))

    c3_all = remote(y.at[others], yr.at[others], c3s.at[0], c3r.at[0], pair)
    loop(1, rooms, lambda d: c3_copy(lax.rem(me + d, rooms)).start())
    yr[me] = y[me]

    pair_copy.wait_recv()

    def g2_wait(k):
        @pl.when((k != g) | (h != core))
        def _():
            g2_arrival(k).wait_recv()

    def squares_of_group(m):
        loop(4 * m, 4 * m + 4, g2_wait)
        for r in range(4):
            for q in range(4):
                pieces = [gf[4 * m + r, k].astype(jnp.float32) for k in range(n // 2 + 1)]
                for tile in range(3):
                    strip = jnp.zeros((16, 128), jnp.float32)
                    for k in range(4):
                        s = 4 * tile + k - r
                        if 0 <= s <= n // 2:
                            turn = (rb * (k - q)) % 128
                            moved = pltpu.roll(pieces[s], turn, 1) if turn else pieces[s]
                            strip = jnp.where(quarter == k, moved, strip)
                    low = 128 * (q // 2) + rb * r + 16 * (q % 2)
                    gs[low : low + 16, 128 * tile : 128 * tile + 128] = strip.astype(jnp.bfloat16)
        wide_low = pl.ds(pl.multiple_of(128 * m, 128), 128)
        wide_high = pl.ds(pl.multiple_of(half + 128 * m, 128), 128)
        for frames, sums in ((c_pair, ms_send), (c_own, ms_own)):
            part = jnp.concatenate([frames[:, wide_low], frames[:, wide_high]], axis=1)
            out = jnp.dot(part, gs[...], preferred_element_type=jnp.float32)
            for tile in range(3):
                cols = pl.ds(pl.multiple_of(core * half + 128 * lax.rem(m + tile, n // 4), 128), 128)
                sums[...] += out[:, 128 * tile : 128 * tile + 128] * frames[:, cols].astype(jnp.float32)

    ms_send[...] = jnp.zeros_like(ms_send)
    ms_own[...] = jnp.zeros_like(ms_own)
    loop(0, n // 4, squares_of_group)
    ms_copy = remote(ms_send, ms_recv, xs.at[1], xr.at[1], pair)
    ms_copy.start()

    for k in range(3):
        w1_copy(k).wait_send()
        m1_copy(k).wait_send()
    for k in range(4):
        w2_each(k, lambda copy: copy.wait_send())
        m2_each(k, lambda copy: copy.wait_send())
    loop(1, n, lambda d: ws_copy(lax.rem(g + d, n)).wait_send())

    @pl.when(shift <= n // 2)
    def _():
        loop(1, n, lambda d: g1_copy(lax.rem(z + d, n)).wait_send())

    c1_all.wait_send()
    loop(0, n, g2_each(lambda copy: copy.wait_send()))
    pair_copy.wait_send()

    ms_copy.wait()
    square_sum = jnp.sum(ms_own[...] + ms_recv[...], axis=1, keepdims=True)
    mean_square = jnp.maximum(square_sum, 0.0) / head_ref.shape[0]
    scale = lax.rsqrt(mean_square + norm_epsilon)
    take = (
        lax.broadcasted_iota(jnp.int32, (rows, rooms * width), 1).astype(jnp.float32)
        == slot_col[:, :1]
    ).astype(jnp.bfloat16)
    c3_all.wait_recv()
    found = jnp.dot(take, yr[...].reshape(rooms * width, -1), preferred_element_type=jnp.float32)
    out_ref[...] = (found * scale).astype(jnp.bfloat16)
    c3_all.wait_send()


def body(raw_clips, clip_lengths, clip_routes, w_spectral, norm_gain, room_heads):
    _, clip_count, slots, window = raw_clips.shape
    n = lax.axis_size("grp")
    rooms = lax.axis_size("fsdp")
    rows = clip_count * slots
    bins = window // 2
    rb, kc = w_spectral.shape
    curve = room_heads.shape[2]
    width = SLOTS * slots

    bf16, f32 = jnp.bfloat16, jnp.float32
    vmem, sems = pltpu.VMEM, lambda k: pltpu.SemaphoreType.DMA((k,))
    coarse = window // 64
    operands = (
        raw_clips.reshape(rows, window),
        w_spectral,
        norm_gain.reshape(1, -1),
        room_heads[0],
        clip_lengths.reshape(1, clip_count),
        clip_routes.reshape(1, clip_count),
    )
    out = pl.pallas_call(
        functools.partial(kernel, n),
        out_shape=jax.ShapeDtypeStruct((rows, curve), bf16),
        in_specs=[pl.BlockSpec(memory_space=pltpu.HBM)] * 6,
        out_specs=pl.BlockSpec(memory_space=pltpu.VMEM),
        scratch_shapes=[
            vmem((rows, window), bf16),
            vmem((rb, kc), bf16),
            vmem((1, n * kc), f32),
            vmem((n * kc, curve), bf16),
            vmem((1, clip_count), jnp.int32),
            vmem((1, clip_count), jnp.int32),
            sems(6),
            vmem((window, 2 * bins), bf16),
            vmem((coarse + 16, bins + 128), f32),
            vmem((coarse + 16, bins + 128), f32),
            vmem((rows, 128), f32),
            vmem((8, rows), f32),
            vmem((rows, 128), f32),
            vmem((rows, bins), bf16),
            vmem((rows, bins), bf16),
            vmem((rooms, width, bins), bf16),
            vmem((rooms, width, bins), bf16),
            vmem((3, rb, kc), bf16),
            vmem((n, 2, rb, kc), bf16),
            vmem((n, rb, kc), bf16),
            vmem((2 * rb, curve), bf16),
            vmem((3, 2 * rb, curve), bf16),
            vmem((n, 2 * rb, curve), bf16),
            vmem((16, 128), bf16),
            vmem((n // 2 + 1, 16, 128), bf16),
            vmem((256, 384), bf16),
            vmem((n, n // 2 + 1, 16, 128), bf16),
            vmem((rooms, width, curve), bf16),
            vmem((rooms, width, curve), bf16),
            vmem((rows, 128), f32),
            vmem((rows, 128), f32),
            vmem((rows, 128), f32),
            sems(3), sems(3), sems(n), sems(n),
            sems(rooms), sems(rooms),
            sems(3), sems(3), sems(16), sems(n),
            sems(n), sems(n), sems(n), sems(n),
            sems(1), sems(1), sems(1), sems(1),
            sems(2), sems(2),
        ],
        compiler_params=pltpu.CompilerParams(
            collective_id=0, has_side_effects=True, vmem_limit_bytes=32 * 2**20
        ),
    )(
        *(pltpu.with_memory_space_constraint(x, pltpu.HBM) for x in operands)
    )
    return out.reshape(1, clip_count, slots, curve)


def solution(mesh):
    return jax.shard_map(
        body,
        mesh=mesh,
        in_specs=(
            P("grp", "fsdp", None, None),
            P("grp", "fsdp", None),
            P("grp", "fsdp", None),
            P("fsdp", "grp"),
            P(),
            P("fsdp", None, None),
        ),
        out_specs=P("grp", "fsdp", None, None),
        check_vma=False,
    )
```

```python
import functools
import math

import jax
import jax.numpy as jnp
from jax import lax
from jax.experimental import pallas as pl
from jax.experimental.pallas import tpu as pltpu
from jax.sharding import PartitionSpec as P

SLOTS = 2
MESH = pl.DeviceIdType.MESH
norm_epsilon = 1e-05


def remote(src, dst, send_sem, recv_sem, device):
    return pltpu.make_async_remote_copy(
        src_ref=src,
        dst_ref=dst,
        send_sem=send_sem,
        recv_sem=recv_sem,
        device_id=device,
        device_id_type=MESH,
    )


def loop(low, high, step):
    def body(i, carry):
        step(i)
        return carry

    lax.fori_loop(low, high, body, 0)


def kernel(
    n,
    raw_hbm, w_hbm, gain_hbm, head_hbm, len_hbm, route_hbm,
    out_ref,
    raw_ref, w_ref, gain_ref, head_ref, len_ref, route_ref, loads,
    tab, trc, trs, slot_col, slot_row, weight, c_own, c_pair, cs, cr, wz, wr, ws, mc, mz, mr,
    gp, gz, gs, gf, y, yr, ms_send, ms_own, ms_recv,
    w1s, w1r, wss, wsr, w2s, w2r, m1s, m1r, m2s, m2r, g1s, g1r, g2s, g2r, c1s, c1r, c3s, c3r, xs, xr,
):
    rooms = 2 * n
    rows, window = raw_ref.shape
    bins = c_own.shape[1]
    half = bins // 2
    rb = w_ref.shape[0]
    g, f = lax.axis_index("grp"), lax.axis_index("fsdp")
    z, h = f // 2, lax.rem(f, 2)
    core = lax.rem(g, 2)
    me = 2 * g + h
    pair = (g + 1 - 2 * core, f)

    def in_plane(q):
        return (q // 2, 2 * z + lax.rem(q, 2))

    def in_column(q):
        return (g, 2 * q + h)

    barrier = pltpu.get_barrier_semaphore()
    placed = ((w_hbm, w_ref), (len_hbm, len_ref), (route_hbm, route_ref), (raw_hbm, raw_ref), (head_hbm, head_ref), (gain_hbm, gain_ref))
    load = [pltpu.make_async_copy(src, dst, loads.at[k]) for k, (src, dst) in enumerate(placed)]
    load[0].start()

    def greet_plane(d):
        pl.semaphore_signal(barrier, inc=1, device_id=in_plane(lax.rem(me + d, rooms)), device_id_type=MESH)

    def greet_column(d):
        pl.semaphore_signal(barrier, inc=1, device_id=in_column(lax.rem(z + d, n)), device_id_type=MESH)

    back = lax.rem(z - g + 2 * n + 1, 4) - 1
    from_plane = lax.rem(z - back + 4 * lax.rem(g, 2) * ((back + 1) // 3) + n, n)

    def greet_senders(q):
        pl.semaphore_signal(barrier, inc=1, device_id=(q // 2, 2 * from_plane + lax.rem(q, 2)), device_id_type=MESH)

    greet_column(n // 2)
    loop(1, n // 2, lambda d: (greet_column(n // 2 - d), greet_column(n // 2 + d)))

    @pl.when(back != 0)
    def _():
        loop(0, rooms, greet_senders)

    loop(1, rooms, greet_plane)
    for copy in load[1:]:
        copy.start()
    load[0].wait()
    pl.semaphore_wait(barrier, rooms - 1 + n - 1 + 3 * 4 * 2)

    far = (n // 2, n // 4, 3 * n // 4)

    def w1_copy(k):
        return remote(w_ref, wz.at[k], w1s.at[k], w1r.at[k], in_column(lax.rem(z + far[k], n)))

    def ws_copy(q):
        return remote(w_ref, ws.at[g], wss.at[q], wsr.at[g], (q, f))

    def ws_arrival(q):
        return remote(w_ref, ws.at[q], wss.at[q], wsr.at[q], (q, f))

    for k in range(3):
        w1_copy(k).start()

    near = (n + 2 - 4 * lax.rem(z, 2), 1, n - 1, 0)

    def w2_each(k, act):
        src = w_ref if k == 3 else wz.at[k]
        origin = z if k == 3 else lax.rem(z + n - far[k], n)
        for e in range(4):
            for side in range(2):
                plane = lax.rem(z + near[e], n)
                copy = remote(
                    src, wr.at[g, h], w2s.at[8 * k + 2 * e + side], w2r.at[me], (origin, 2 * plane + side)
                )
                if e < 3:
                    act(copy)
                else:

                    @pl.when((origin != g) | (h != side))
                    def _():
                        act(copy)

    def w2_arrival(q):
        return remote(w_ref, wr.at[q // 2, lax.rem(q, 2)], w2s.at[0], w2r.at[q], in_plane(q))

    w2_each(3, lambda copy: copy.start())
    loop(1, n, lambda d: ws_copy(lax.rem(g + d, n)).start())
    ws[g] = w_ref[...]

    load[1].wait()
    load[2].wait()

    clips = len_ref.shape[1]
    row = lax.broadcasted_iota(jnp.int32, (rows, clips), 0)
    other = lax.broadcasted_iota(jnp.int32, (rows, clips), 1)
    lengths = jnp.broadcast_to(len_ref[...].astype(jnp.float32), (rows, clips))
    routes = jnp.broadcast_to(route_ref[...].astype(jnp.float32), (rows, clips))

    def total(kept, of):
        return jnp.sum(jnp.where(kept, of, 0.0), axis=1, keepdims=True)

    length = total(other == row // 8, lengths)
    route = total(other == row // 8, routes)
    rank = total((other < row // 8) & (routes == route), jnp.ones_like(routes))
    frame = (lax.broadcasted_iota(jnp.int32, (rows, 1), 0) % 8).astype(jnp.float32)
    slot = jnp.where(frame < length, (route * SLOTS + rank) * 8.0 + frame, -1.0)
    slot_all = jnp.broadcast_to(slot, (rows, 128))
    slot_col[...] = slot_all
    slot_row[...] = jnp.transpose(slot_all)[:8, :]
    weight[...] = jnp.broadcast_to(jnp.where(frame < length, 1.0 / length, 0.0), (rows, 128))

    wide = bins + 128
    coarse = window // 64
    lane = lax.broadcasted_iota(jnp.int32, (8, wide), 1)
    bin_idx = jnp.where(
        lane < bins, 2 * rb * ((lane % half) // rb) + rb * (lane // half) + lane % rb, 1
    )
    sub = lax.broadcasted_iota(jnp.int32, (8, wide), 0)

    def trig_rows(base, factor, first):
        angle = (((sub + first) * factor * bin_idx) & (window - 1)).astype(jnp.float32) * (
            2.0 * math.pi / window
        )
        trc[pl.ds(base, 8), :] = jnp.cos(angle)
        trs[pl.ds(base, 8), :] = jnp.sin(angle)

    loop(0, coarse // 8, lambda i: trig_rows(pl.multiple_of(8 * i, 8), 64, 8 * i))
    trig_rows(coarse, 8, 0)
    trig_rows(coarse + 8, 1, 0)

    def table_rows(a):
        ac, as_ = trc[pl.ds(a, 1), :], trs[pl.ds(a, 1), :]
        bc, bs = trc[coarse : coarse + 8, :], trs[coarse : coarse + 8, :]
        cc, cs_ = trc[coarse + 8 : coarse + 16, :], trs[coarse + 8 : coarse + 16, :]
        mid_c = ac * bc - as_ * bs
        mid_s = as_ * bc + ac * bs
        for b in range(0, 8, 2):
            real, imag = [], []
            for e in (b, b + 1):
                c1, s1 = mid_c[e : e + 1, :], mid_s[e : e + 1, :]
                cosines = c1 * cc - s1 * cs_
                sines = s1[:, :bins] * cc[:, :bins] + c1[:, :bins] * cs_[:, :bins]
                taper = 0.5 - 0.5 * cosines[:, bins:]
                taper = jnp.concatenate([taper] * (bins // 128), axis=1)
                real.append(taper * cosines[:, :bins])
                imag.append(-(taper * sines))
            here = pl.ds(pl.multiple_of(64 * a + 8 * b, 16), 16)
            tab[here, :bins] = jnp.concatenate(real, axis=0).astype(jnp.bfloat16)
            tab[here, bins:] = jnp.concatenate(imag, axis=0).astype(jnp.bfloat16)

    loop(0, coarse, table_rows)

    for k in range(3):
        w1_copy(k).wait_recv()
        w2_each(k, lambda copy: copy.start())

    @pl.when(back == 0)
    def _():
        for k in range(4):
            origin = z if k == 3 else lax.rem(z + n - far[k], n)

            @pl.when(origin == g)
            def _():
                wr[g, h] = w_ref[...] if k == 3 else wz[k]

    block = min(256, bins)

    def spectra_block(i):
        here = pl.ds(pl.multiple_of(i * block, block), block)
        there = pl.ds(pl.multiple_of(bins + i * block, block), block)
        frames = raw_ref[...]
        re = jnp.dot(frames, tab[:, here], preferred_element_type=jnp.float32)
        im = jnp.dot(frames, tab[:, there], preferred_element_type=jnp.float32)
        energy = jnp.log1p((re * re + im * im) / window)
        kept = (energy * weight[:, :1]).reshape(rows // 8, 8, block)
        mean = jnp.sum(kept, axis=1, keepdims=True)
        centered = energy.reshape(rows // 8, 8, block) - mean
        c_own[:, here] = centered.reshape(rows, block).astype(jnp.bfloat16)

    load[3].wait()
    loop(0, bins // block, spectra_block)

    pair_copy = remote(c_own, c_pair, xs.at[0], xr.at[0], pair)
    pair_copy.start()

    width = cs.shape[1]
    place = (
        lax.broadcasted_iota(jnp.int32, (rooms * width, rows), 0).astype(jnp.float32)
        == slot_row[:1, :]
    ).astype(jnp.bfloat16)

    def place_block(i):
        here = pl.ds(pl.multiple_of(i * block, block), block)
        spread = jnp.dot(place, c_own[:, here], preferred_element_type=jnp.float32)
        cs[:, :, here] = spread.astype(jnp.bfloat16).reshape(rooms, width, block)

    loop(0, bins // block, place_block)

    def c1_copy(q):
        return remote(cs.at[q], cr.at[me], c1s.at[0], c1r.at[0], in_plane(q))

    others = pl.ds(0, rooms - 1)
    c1_all = remote(cs.at[others], cr.at[others], c1s.at[0], c1r.at[0], pair)
    loop(1, rooms, lambda d: c1_copy(lax.rem(me + d, rooms)).start())
    cr[me] = cs[me]

    def w2_wait(q):
        @pl.when((q != me) | (back != 0))
        def _():
            w2_arrival(q).wait_recv()

    loop(0, rooms, w2_wait)
    loop(1, n, lambda d: ws_arrival(lax.rem(g + d, n)).wait_recv())

    w_rows = jnp.concatenate([wr[k].reshape(2 * rb, -1) for k in range(n)], axis=1)
    load[4].wait()
    load[5].wait()
    scaled = w_rows.astype(jnp.float32) * gain_ref[...]
    scaled_high = scaled.astype(jnp.bfloat16)
    scaled_low = (scaled - scaled_high.astype(jnp.float32)).astype(jnp.bfloat16)
    both = jnp.concatenate([scaled_high, scaled_low], axis=0)
    product = jnp.dot(both, head_ref[...], preferred_element_type=jnp.float32)
    mc[...] = (product[: 2 * rb] + product[2 * rb :]).astype(jnp.bfloat16)

    def m1_copy(k):
        return remote(mc, mz.at[k], m1s.at[k], m1r.at[k], in_column(lax.rem(z + far[k], n)))

    def m2_each(k, act):
        src = mc if k == 3 else mz.at[k]
        origin = z if k == 3 else lax.rem(z + n - far[k], n)
        for e in range(4):
            plane = lax.rem(z + near[e], n)
            copy = remote(src, mr.at[g], m2s.at[4 * k + e], m2r.at[g], (origin, 2 * plane + h))
            if e < 3:
                act(copy)
            else:

                @pl.when(origin != g)
                def _():
                    act(copy)

    def m2_arrival(q):
        return remote(mc, mr.at[q], m2s.at[0], m2r.at[q], (q, f))

    for k in range(3):
        m1_copy(k).start()
    m2_each(3, lambda copy: copy.start())
    w_cols = jnp.concatenate([ws[k] for k in range(n)], axis=1)
    gram = lax.dot_general(
        w_rows,
        jnp.concatenate([w_cols] * 4, axis=0),
        (((1,), (1,)), ((), ())),
        preferred_element_type=jnp.float32,
    )
    quarter = lax.broadcasted_iota(jnp.int32, (16, 128), 1) // rb
    piece = jnp.zeros((16, 128), jnp.float32)
    for q in range(4):
        piece = jnp.where(quarter == q, gram[16 * q : 16 * q + 16, :], piece)
    shift = lax.rem(z - g + n, n)
    twice = jnp.where((shift > 0) & (shift < n // 2), 2.0, 1.0)
    gp[...] = (piece * twice).astype(jnp.bfloat16)

    def g1_copy(q):
        return remote(gp, gz.at[shift], g1s.at[q], g1r.at[shift], in_column(q))

    def g1_arrival(k):
        return remote(gp, gz.at[k], g1s.at[0], g1r.at[k], in_column(lax.rem(g + k, n)))

    @pl.when(shift <= n // 2)
    def _():
        loop(1, n, lambda d: g1_copy(lax.rem(z + d, n)).start())
        gz[shift] = gp[...]

    for k in range(3):
        m1_copy(k).wait_recv()
        m2_each(k, lambda copy: copy.start())

    @pl.when(back == 0)
    def _():
        for k in range(4):
            origin = z if k == 3 else lax.rem(z + n - far[k], n)

            @pl.when(origin == g)
            def _():
                mr[g] = mc[...] if k == 3 else mz[k]

    def g1_wait(k):
        @pl.when(k != shift)
        def _():
            g1_arrival(k).wait_recv()

    loop(0, n // 2 + 1, g1_wait)

    def g2_copy(q):
        return remote(gz, gf.at[g], g2s.at[q], g2r.at[g], (2 * (q // 2) + h, 2 * z + lax.rem(q, 2)))

    def g2_arrival(k):
        return remote(gz, gf.at[k], g2s.at[0], g2r.at[k], (k, 2 * z + core))

    own = 2 * (g // 2) + h

    def g2_each(act):
        def step(d):
            q = lax.rem(own + n // 2 + d, n)

            @pl.when((2 * (q // 2) + h != g) | (lax.rem(q, 2) != h))
            def _():
                act(g2_copy(q))

        return step

    loop(0, n, g2_each(lambda copy: copy.start()))

    @pl.when(h == core)
    def _():
        gf[g] = gz[...]

    c1_all.wait_recv()
    def m2_wait(q):
        @pl.when((q != g) | (back != 0))
        def _():
            m2_arrival(q).wait_recv()

    loop(0, n, m2_wait)
    low = mr[:, :rb, :].reshape(half, -1)
    high = mr[:, rb:, :].reshape(half, -1)
    got = cr[...].reshape(rooms * width, bins)
    curves = jnp.dot(got[:, :half], low, preferred_element_type=jnp.float32)
    curves = curves + jnp.dot(got[:, half:], high, preferred_element_type=jnp.float32)
    y[...] = curves.astype(jnp.bfloat16).reshape(y.shape)

    def c3_copy(q):
        return remote(y.at[q], yr.at[me], c3s.at[0], c3r.at[0], in_plane(q))

    c3_all = remote(y.at[others], yr.at[others], c3s.at[0], c3r.at[0], pair)
    loop(1, rooms, lambda d: c3_copy(lax.rem(me + d, rooms)).start())
    yr[me] = y[me]

    pair_copy.wait_recv()

    def g2_wait(k):
        @pl.when((k != g) | (h != core))
        def _():
            g2_arrival(k).wait_recv()

    def squares_of_group(m):
        loop(4 * m, 4 * m + 4, g2_wait)
        for r in range(4):
            for q in range(4):
                pieces = [gf[4 * m + r, k].astype(jnp.float32) for k in range(n // 2 + 1)]
                for tile in range(3):
                    strip = jnp.zeros((16, 128), jnp.float32)
                    for k in range(4):
                        s = 4 * tile + k - r
                        if 0 <= s <= n // 2:
                            turn = (rb * (k - q)) % 128
                            moved = pltpu.roll(pieces[s], turn, 1) if turn else pieces[s]
                            strip = jnp.where(quarter == k, moved, strip)
                    low = 128 * (q // 2) + rb * r + 16 * (q % 2)
                    gs[low : low + 16, 128 * tile : 128 * tile + 128] = strip.astype(jnp.bfloat16)
        wide_low = pl.ds(pl.multiple_of(128 * m, 128), 128)
        wide_high = pl.ds(pl.multiple_of(half + 128 * m, 128), 128)
        for frames, sums in ((c_pair, ms_send), (c_own, ms_own)):
            part = jnp.concatenate([frames[:, wide_low], frames[:, wide_high]], axis=1)
            out = jnp.dot(part, gs[...], preferred_element_type=jnp.float32)
            for tile in range(3):
                cols = pl.ds(pl.multiple_of(core * half + 128 * lax.rem(m + tile, n // 4), 128), 128)
                sums[...] += out[:, 128 * tile : 128 * tile + 128] * frames[:, cols].astype(jnp.float32)

    ms_send[...] = jnp.zeros_like(ms_send)
    ms_own[...] = jnp.zeros_like(ms_own)
    loop(0, n // 4, squares_of_group)
    ms_copy = remote(ms_send, ms_recv, xs.at[1], xr.at[1], pair)
    ms_copy.start()

    for k in range(3):
        w1_copy(k).wait_send()
        m1_copy(k).wait_send()
    for k in range(4):
        w2_each(k, lambda copy: copy.wait_send())
        m2_each(k, lambda copy: copy.wait_send())
    loop(1, n, lambda d: ws_copy(lax.rem(g + d, n)).wait_send())

    @pl.when(shift <= n // 2)
    def _():
        loop(1, n, lambda d: g1_copy(lax.rem(z + d, n)).wait_send())

    c1_all.wait_send()
    loop(0, n, g2_each(lambda copy: copy.wait_send()))
    pair_copy.wait_send()

    ms_copy.wait()
    square_sum = jnp.sum(ms_own[...] + ms_recv[...], axis=1, keepdims=True)
    mean_square = jnp.maximum(square_sum, 0.0) / head_ref.shape[0]
    scale = lax.rsqrt(mean_square + norm_epsilon)
    take = (
        lax.broadcasted_iota(jnp.int32, (rows, rooms * width), 1).astype(jnp.float32)
        == slot_col[:, :1]
    ).astype(jnp.bfloat16)
    c3_all.wait_recv()
    found = jnp.dot(take, yr[...].reshape(rooms * width, -1), preferred_element_type=jnp.float32)
    out_ref[...] = (found * scale).astype(jnp.bfloat16)
    c3_all.wait_send()


def body(raw_clips, clip_lengths, clip_routes, w_spectral, norm_gain, room_heads):
    _, clip_count, slots, window = raw_clips.shape
    n = lax.axis_size("grp")
    rooms = lax.axis_size("fsdp")
    rows = clip_count * slots
    bins = window // 2
    rb, kc = w_spectral.shape
    curve = room_heads.shape[2]
    width = SLOTS * slots

    bf16, f32 = jnp.bfloat16, jnp.float32
    vmem, sems = pltpu.VMEM, lambda k: pltpu.SemaphoreType.DMA((k,))
    coarse = window // 64
    operands = (
        raw_clips.reshape(rows, window),
        w_spectral,
        norm_gain.reshape(1, -1),
        room_heads[0],
        clip_lengths.reshape(1, clip_count),
        clip_routes.reshape(1, clip_count),
    )
    out = pl.pallas_call(
        functools.partial(kernel, n),
        out_shape=jax.ShapeDtypeStruct((rows, curve), bf16),
        in_specs=[pl.BlockSpec(memory_space=pltpu.HBM)] * 6,
        out_specs=pl.BlockSpec(memory_space=pltpu.VMEM),
        scratch_shapes=[
            vmem((rows, window), bf16),
            vmem((rb, kc), bf16),
            vmem((1, n * kc), f32),
            vmem((n * kc, curve), bf16),
            vmem((1, clip_count), jnp.int32),
            vmem((1, clip_count), jnp.int32),
            sems(6),
            vmem((window, 2 * bins), bf16),
            vmem((coarse + 16, bins + 128), f32),
            vmem((coarse + 16, bins + 128), f32),
            vmem((rows, 128), f32),
            vmem((8, rows), f32),
            vmem((rows, 128), f32),
            vmem((rows, bins), bf16),
            vmem((rows, bins), bf16),
            vmem((rooms, width, bins), bf16),
            vmem((rooms, width, bins), bf16),
            vmem((3, rb, kc), bf16),
            vmem((n, 2, rb, kc), bf16),
            vmem((n, rb, kc), bf16),
            vmem((2 * rb, curve), bf16),
            vmem((3, 2 * rb, curve), bf16),
            vmem((n, 2 * rb, curve), bf16),
            vmem((16, 128), bf16),
            vmem((n // 2 + 1, 16, 128), bf16),
            vmem((256, 384), bf16),
            vmem((n, n // 2 + 1, 16, 128), bf16),
            vmem((rooms, width, curve), bf16),
            vmem((rooms, width, curve), bf16),
            vmem((rows, 128), f32),
            vmem((rows, 128), f32),
            vmem((rows, 128), f32),
            sems(3), sems(3), sems(n), sems(n),
            sems(rooms), sems(rooms),
            sems(3), sems(3), sems(16), sems(n),
            sems(n), sems(n), sems(n), sems(n),
            sems(1), sems(1), sems(1), sems(1),
            sems(2), sems(2),
        ],
        compiler_params=pltpu.CompilerParams(
            collective_id=0, has_side_effects=True, vmem_limit_bytes=32 * 2**20
        ),
    )(
        *(pltpu.with_memory_space_constraint(x, pltpu.HBM) for x in operands)
    )
    return out.reshape(1, clip_count, slots, curve)


def solution(mesh):
    return jax.shard_map(
        body,
        mesh=mesh,
        in_specs=(
            P("grp", "fsdp", None, None),
            P("grp", "fsdp", None),
            P("grp", "fsdp", None),
            P("fsdp", "grp"),
            P(),
            P("fsdp", None, None),
        ),
        out_specs=P("grp", "fsdp", None, None),
        check_vma=False,
    )
```
